256 devices in a mesh: occi: 4 (over x_hi, core), occj: 8 (over z), virt: 8 (over x_lo, y).
Axes of the slice: x: 4 (x_hi: 2, x_lo: 2; x = x_hi * 2 + x_lo), y: 4, z: 8, core: 2. Of those that a mesh axis runs over, the one named last changes fastest.
Arguments:
- amplitude: bfloat16 [80, 80, 4, 16384], P('occi', 'occj', None, 'virt'), may hold values from -6 to 6
- integral: bfloat16 [4, 16384, 2048], P('occi', 'virt'), may hold values from -0.046875 to 0.046875
- tile_mask: int32 [80, 4, 128], P('occi', None, 'virt'), may hold values 0 or 1
- pair_irrep: int32 [4, 128], P('occi', 'virt'), may hold values from 0 to 3
- slice_irrep: int32 [16], replicated, may hold values from 0 to 3
- integral_mask: int32 [4, 128, 16], P('occi', 'virt'), may hold values 0 or 1
Outputs:
- residual: bfloat16 [80, 80, 2048], P('occi', 'occj', 'virt')
The draws below stay inside these ranges and needn't reach their ends.
All inputs are finite; a program needn't handle non-finite values. No bound on the sum of `tile_mask` or of `integral_mask` on one device may be relied on, other than what follows from the above.
Results may differ from the reference program's by a relative error of at most 0.022.
Values may be sent and summed in bfloat16 or wider, within the bound.
A program may use at most 128 MiB of HBM per device.

```python
import jax
import jax.numpy as jnp
from jax import lax

O = 80
VB = 128
NIRREP = 4
CD_DEV = 2048
AB_BLK = 16
AB = 2048
QUART = 4
CD4 = 16384
NCB4 = 128
CD = 65536


def plant(values, rng, low, high):
    index_at = [jax.random.randint(jax.random.fold_in(rng, axis), (), 0, length) for axis, length in enumerate(values.shape)]
    widest = values.shape.index(max(values.shape))
    neighbour = index_at[:widest] + [(index_at[widest] + 1) % values.shape[widest]] + index_at[widest + 1:]
    return values.at[tuple(index_at)].set(low).at[tuple(neighbour)].set(high)


def block_levels(own_key, dims, cuts, low, largest):
    def one(axis_at, parts):
        steps = jax.random.uniform(jax.random.fold_in(jax.random.fold_in(own_key, 6), axis_at), (parts,), jnp.float32, low / len(cuts), largest / len(cuts))
        return jnp.repeat(jnp.exp(steps), dims[axis_at] // parts).reshape((-1,) + (1,) * (len(dims) - axis_at - 1))

    factor_of = one(*cuts[0])
    for cut in cuts[1:]:
        factor_of = factor_of * one(*cut)
    return factor_of


def bell_draw(stream_key, shape, spread, bound, pieces=(), dtype=jnp.bfloat16):
    array = jax.random.normal(stream_key, shape, jnp.float32) * spread
    if len(pieces) > 0:
        array = block_levels(stream_key, shape, pieces, -0.22, 0.18) * array
    return jnp.clip(array, min=-bound, max=bound).astype(dtype)


def setup_inputs(seed: int = 0) -> dict:
    seeds = jax.random.split(jax.random.key(seed), 7)
    amplitude = bell_draw(seeds[0], (O, O, QUART, CD4), 1.0, 6.0, ((0, 4), (1, 8), (3, 8)))
    integral = bell_draw(seeds[1], (QUART, CD4, AB), (CD // 4) ** -0.5, 0.046875, ((0, 4), (1, 8)))
    tile_mask = plant((jax.random.randint(seeds[2], (O, QUART, NCB4), 0, 4) < 3).astype(jnp.int32), jax.random.fold_in(seeds[2], 1), 0, 1)
    pair_irrep = plant(jax.random.randint(seeds[3], (QUART, NCB4), 0, NIRREP), jax.random.fold_in(seeds[3], 1), 0, NIRREP - 1).astype(jnp.int32)
    slice_irrep = plant(jax.random.randint(seeds[4], (AB_BLK,), 0, NIRREP), jax.random.fold_in(seeds[4], 1), 0, NIRREP - 1).astype(jnp.int32)
    integral_mask = plant((jax.random.randint(seeds[5], (QUART, NCB4, AB_BLK), 0, 4) < 3).astype(jnp.int32), jax.random.fold_in(seeds[5], 1), 0, 1)
    return dict(amplitude=amplitude, integral=integral, tile_mask=tile_mask, pair_irrep=pair_irrep, slice_irrep=slice_irrep, integral_mask=integral_mask)


def swap_pairs(field):
    shape = field.shape
    halves = field.reshape(shape[0], shape[1], shape[2] // 2, 2)
    return halves[..., ::-1].reshape(shape)


def reference(amplitude, integral, tile_mask, pair_irrep, slice_irrep, integral_mask):
    col_mask = jnp.broadcast_to(tile_mask[:, :, :, None], (O, QUART, NCB4, VB)).reshape(O, 1, QUART, CD4)
    masked = (amplitude * col_mask.astype(jnp.bfloat16)).reshape(O * O, CD)
    keep = (pair_irrep.reshape(-1)[:, None] == slice_irrep[None, :]) * integral_mask.reshape(CD // VB, AB_BLK)
    weights = integral.reshape(CD // VB, VB, AB_BLK, VB) * keep[:, None, :, None].astype(jnp.bfloat16)
    effective = weights.reshape(CD, AB)
    width = CD_DEV

    def add_block(index, total):
        start = (index * width).astype(jnp.int32)
        left = lax.dynamic_slice_in_dim(masked, start, width, 1)
        right = lax.dynamic_slice_in_dim(effective, start, width, 0)
        term = jnp.dot(left, right, preferred_element_type=jnp.float32).astype(jnp.bfloat16)
        term = lax.optimization_barrier(term)
        return total + term.astype(jnp.float32)

    ladder = lax.fori_loop(0, CD // width, add_block, jnp.zeros((O * O, AB), jnp.float32))
    ladder = ladder.reshape(O, O, AB)
    mirror = swap_pairs(jnp.transpose(ladder, (1, 0, 2)))
    return (ladder + mirror).astype(jnp.bfloat16)
```

```python
import jax
import jax.numpy as jnp
from jax import lax
from jax.experimental import pallas as pl
from jax.experimental.pallas import tpu as pltpu
from jax.sharding import PartitionSpec as P

MESH = pl.DeviceIdType.MESH
BF = jnp.bfloat16
F32 = jnp.float32
CH = 5
CR = 40
BL = 16
VB = 128
W = BL * VB
NB = 8
NW = 256
BLK = 112


def iota(shape, axis):
    return lax.broadcasted_iota(jnp.int32, shape, axis)


def matmul(a, b):
    return jnp.dot(a, b, preferred_element_type=F32)


def kernel(
    amp, vint, tm, pi, si, im, out,
    raw, ma, lh, lhs, v, kx, wm, perm, expand, sel, turn, swap,
    pk, cs, cr, ys, yr, xt, xs, xr, total, ts, tr,
    raw_sem, v_sem, a_ss, a_rs, c_ss, c_rs, y_ss, y_rs, x_ss, x_rs, t_ss, t_rs, t_ls,
):
    occi, z, virt = lax.axis_index("occi"), lax.axis_index("occj"), lax.axis_index("virt")
    xh, c = occi // 2, occi % 2
    xl, y = virt // 4, virt % 4

    def dev(h, core, low, yy):
        return (2 * h + core, z, 4 * low + yy)

    sibling = dev(xh, 1 - c, xl, y)
    far_same = dev(1 - xh, c, xl, y)
    far_other = dev(1 - xh, 1 - c, xl, y)
    near = dev(xh, c, 1 - xl, y)
    far_near = dev(1 - xh, c, 1 - xl, y)
    y_peer = [dev(xh, c, xl, (y + d) % 4) for d in (1, 2, 3)]
    turned = [(z // 2, 2 * occi + h, virt) for h in (0, 1)]
    on_diag = (z // 2) == occi
    here = z % 2

    def raw_copy(k, t):
        return pltpu.make_async_copy(
            amp.at[pl.ds(k * CR, CR), t], raw.at[k * BL + t], raw_sem.at[k]
        )

    def start_raw(k, _):
        for t in range(BL):
            raw_copy(k, t).start()
        return 0

    def v_copy(n):
        return pltpu.make_async_copy(
            vint.at[0, :, pl.ds(pl.multiple_of(n * NW, NW), NW)], v.at[n], v_sem.at[n]
        )

    def start_v(n, _):
        v_copy(n).start()
        return 0

    lax.fori_loop(0, CH, start_raw, 0)
    lax.fori_loop(0, NB, start_v, 0)

    barrier = pltpu.get_barrier_semaphore()
    for peer in [sibling, far_same, far_other, near, far_near] + y_peer:
        pl.semaphore_signal(barrier, inc=1, device_id=peer, device_id_type=MESH)
    for h in (0, 1):
        @pl.when(jnp.logical_not(jnp.logical_and(on_diag, here == h)))
        def _():
            pl.semaphore_signal(barrier, inc=1, device_id=turned[h], device_id_type=MESH)

    row, col = iota((4 * CR, 4 * CR), 0), iota((4 * CR, 4 * CR), 1)
    perm[...] = jnp.where(col == (row % CR) * 4 + row // CR, 1.0, 0.0).astype(BF)
    expand[...] = jnp.where(iota((BL, W), 1) // VB == iota((BL, W), 0), 1.0, 0.0).astype(BF)
    ri, ci = iota((CH * CR, 20), 0), iota((CH * CR, 20), 1)
    own_i = jnp.where(ri // 10 == ci, 1.0, 0.0).astype(BF)
    for q in range(4):
        flags = lax.dot_general(
            own_i, tm[q].astype(F32).astype(BF), (((1,), (1,)), ((), ())),
            preferred_element_type=F32,
        )
        for k in range(CH):
            wm[k, q * CR:(q + 1) * CR, :] = flags[k * CR:(k + 1) * CR, :]

    def a_copies(k):
        far_q = 2 * (1 - xh)
        plan = (
            (0, far_q + c, CH + k, 0, far_same),
            (1, far_q + 1 - c, CH + k, 1, far_other),
            (2, 2 * xh + 1 - c, k, 1, sibling),
        )
        return [
            pltpu.make_async_remote_copy(
                src_ref=ma.at[q, k], dst_ref=lh.at[s, side],
                send_sem=a_ss.at[k, n], recv_sem=a_rs.at[k, n],
                device_id=peer, device_id_type=MESH,
            )
            for n, q, s, side, peer in plan
        ]

    rawf = raw.reshape(CH * BL, 4 * CR, VB)

    def spread(k, _):
        pltpu.make_async_copy(
            raw.at[pl.ds(k * BL, BL)], raw.at[pl.ds(k * BL, BL)], raw_sem.at[k]
        ).wait()
        flags = wm[k].astype(BF)
        for part in range(4):
            x = jnp.concatenate([rawf[k * BL + part * 4 + t] for t in range(4)], axis=1)
            lanes = pl.ds(part * 4 * VB, 4 * VB)
            got = matmul(perm[...], x) * matmul(flags, expand[:, lanes])
            for q in range(4):
                ma[q, k, :, lanes] = got[q * CR:(q + 1) * CR].astype(BF)

        @pl.when(k == 0)
        def _():
            pl.semaphore_wait(barrier, 10 - on_diag.astype(jnp.int32))

        for copy in a_copies(k):
            copy.start()
        lh[k, 0] = ma[2 * xh + c, k]
        return 0

    lax.fori_loop(0, CH, spread, 0)

    eye = iota((BL, BL), 0) == iota((BL, BL), 1)
    own_label = jnp.sum(jnp.where(eye, pi[...], 0), axis=1, keepdims=True)
    keep = jnp.where(own_label == si[...], im[0], 0).astype(F32).astype(BF)
    for n in range(NB):
        kx[n] = matmul(keep, expand[:, n * NW:(n + 1) * NW])

    def mask_v(n, _):
        v_copy(n).wait()
        for b in range(BL):
            line = jnp.broadcast_to(kx[n, b:b + 1, :], (16, NW)).astype(BF)
            rows = pl.ds(b * VB, VB)
            v[n, rows, :] = (v[n, rows, :].reshape(8, 16, NW) * line[None]).reshape(VB, NW)
        return 0

    lax.fori_loop(0, NB, mask_v, 0)

    rs, cs_ = iota((2 * BLK, CH * CR), 0), iota((2 * BLK, CH * CR), 1)
    part_s = rs % BLK
    sel[...] = jnp.where(
        jnp.logical_and(part_s < 100, cs_ == 100 * (rs // BLK) + part_s), 1.0, 0.0
    ).astype(BF)
    rt, ct = iota((CH * CR, 2 * BLK), 0), iota((CH * CR, 2 * BLK), 1)
    it, jt = rt // 10, rt % 10
    turn[...] = jnp.where(ct == BLK * (it // 10) + jt * 10 + it % 10, 1.0, 0.0).astype(BF)
    aw, bw = iota((NW, NW), 0), iota((NW, NW), 1)
    swap[...] = jnp.where(aw == bw + 1 - 2 * (bw % 2), 1.0, 0.0).astype(BF)

    def c_copy(s):
        return pltpu.make_async_remote_copy(
            src_ref=cs.at[s], dst_ref=cr.at[s], send_sem=c_ss.at[s], recv_sem=c_rs.at[s],
            device_id=sibling, device_id_type=MESH,
        )

    def y_copies(s):
        return [
            pltpu.make_async_remote_copy(
                src_ref=ys.at[s, :, (y + d) % 4], dst_ref=yr.at[s, d - 1],
                send_sem=y_ss.at[s, d - 1], recv_sem=y_rs.at[s, d - 1],
                device_id=y_peer[d - 1], device_id_type=MESH,
            )
            for d in (1, 2, 3)
        ]

    def x_copy(s, n, source, low, peer):
        return pltpu.make_async_remote_copy(
            src_ref=xs.at[source, low], dst_ref=xr.at[s, n],
            send_sem=x_ss.at[s, n], recv_sem=x_rs.at[s, n],
            device_id=peer, device_id_type=MESH,
        )

    def x_copies(k):
        return [
            x_copy(k, 0, k, 1 - xl, near),
            x_copy(k, 1, CH + k, xl, far_same),
            x_copy(k, 2, CH + k, 1 - xl, far_near),
        ]

    def multiply(s):
        @pl.when(s < CH)
        def _():
            a_copies(s)[2].wait_recv()

        @pl.when(s >= CH)
        def _():
            a_copies(s - CH)[0].wait_recv()
            a_copies(s - CH)[1].wait_recv()

        lhs[...] = jnp.concatenate(
            [lh[s, 0].astype(F32), lh[s, 1].astype(F32)], axis=0
        ).astype(BF)

        def column(n, _):
            got = matmul(lhs[...], v[n])
            pk[s, n // 4, n % 4] = got[:CR]
            cs[s, n // 4, n % 4] = got[CR:].astype(BF)
            return 0

        lax.fori_loop(0, NB, column, 0)
        c_copy(s).start()

    def over_cores(s):
        c_copy(s).wait_recv()
        for low in range(2):
            for yy in range(4):
                both = pk[s, low, yy] + cr[s, low, yy].astype(F32)
                pk[s, low, yy] = both
                ys[s, low, yy] = both.astype(BF)
        for copy in y_copies(s):
            copy.start()

    def over_y(s):
        for copy in y_copies(s):
            copy.wait_recv()
        for low in range(2):
            both = pk[s, low, y]
            for d in range(3):
                both = both + yr[s, d, low].astype(F32)
            xt[s, low] = both
            xs[s, low] = both.astype(BF)

        @pl.when(s < CH)
        def _():
            x_copies(s)[0].start()

        @pl.when(s >= CH)
        def _():
            x_copies(s - CH)[1].start()
            x_copies(s - CH)[2].start()

    def over_x(k):
        for copy in x_copies(k):
            copy.wait_recv()
        both = xt[k, xl]
        for d in range(3):
            both = both + xr[k, d].astype(F32)
        total[pl.ds(pl.multiple_of(k * CR, 8), CR), :] = both

    def step(s, _):
        multiply(s)
        over_cores(s)

        @pl.when(s >= 1)
        def _():
            over_y(s - 1)

        @pl.when(s >= CH + 2)
        def _():
            over_x(s - CH - 2)

        return 0

    lax.fori_loop(0, 2 * CH, step, 0)
    over_y(2 * CH - 1)
    over_x(CH - 2)
    over_x(CH - 1)

    mirrored = matmul(total[...].astype(BF), swap[...]).astype(BF)
    blocks = matmul(sel[...], mirrored).astype(BF)
    for h in (0, 1):
        ts[h] = blocks[h * BLK:(h + 1) * BLK]

    def t_copy(h):
        return pltpu.make_async_remote_copy(
            src_ref=ts.at[h], dst_ref=tr.at[here], send_sem=t_ss.at[h], recv_sem=t_rs.at[here],
            device_id=turned[h], device_id_type=MESH,
        )

    def t_arrival(h):
        return pltpu.make_async_remote_copy(
            src_ref=ts.at[h], dst_ref=tr.at[h], send_sem=t_ss.at[h], recv_sem=t_rs.at[h],
            device_id=turned[h], device_id_type=MESH,
        )

    def t_local(h):
        return pltpu.make_async_copy(ts.at[h], tr.at[h], t_ls)

    for h in (0, 1):
        mine = jnp.logical_and(on_diag, here == h)

        @pl.when(mine)
        def _():
            t_local(h).start()

        @pl.when(jnp.logical_not(mine))
        def _():
            t_copy(h).start()

    def sent(k, _):
        for copy in a_copies(k) + x_copies(k):
            copy.wait_send()
        return 0

    def sent_sums(s, _):
        for copy in [c_copy(s)] + y_copies(s):
            copy.wait_send()
        return 0

    lax.fori_loop(0, CH, sent, 0)
    lax.fori_loop(0, 2 * CH, sent_sums, 0)

    for h in (0, 1):
        mine = jnp.logical_and(on_diag, here == h)

        @pl.when(mine)
        def _():
            t_local(h).wait()

        @pl.when(jnp.logical_not(mine))
        def _():
            t_arrival(h).wait_recv()
            t_copy(h).wait_send()

    arrived = jnp.concatenate([tr[0], tr[1]], axis=0)
    out[...] = (total[...] + matmul(turn[...], arrived)).astype(BF)


def shards(amplitude, integral, tile_mask, pair_irrep, slice_irrep, integral_mask):
    rows_i, rows_j, groups, width = amplitude.shape
    rows = rows_i * rows_j
    tiles = amplitude.reshape(rows, groups, BL, VB).transpose(0, 2, 1, 3)
    steps = 2 * CH
    dma = pltpu.SemaphoreType.DMA
    vmem = pl.BlockSpec(memory_space=pltpu.VMEM)
    hbm = pl.BlockSpec(memory_space=pl.ANY)
    result = pl.pallas_call(
        kernel,
        out_shape=jax.ShapeDtypeStruct((rows, NW), BF),
        in_specs=[hbm, hbm, vmem, vmem, vmem, vmem],
        out_specs=vmem,
        scratch_shapes=[
            pltpu.VMEM((CH * BL, CR, groups, VB), BF),
            pltpu.VMEM((groups, CH, CR, W), BF),
            pltpu.VMEM((steps, 2, CR, W), BF),
            pltpu.VMEM((2 * CR, W), BF),
            pltpu.VMEM((NB, W, NW), BF),
            pltpu.VMEM((NB, BL, NW), F32),
            pltpu.VMEM((CH, groups * CR, BL), F32),
            pltpu.VMEM((groups * CR, groups * CR), BF),
            pltpu.VMEM((BL, W), BF),
            pltpu.VMEM((2 * BLK, rows), BF),
            pltpu.VMEM((rows, 2 * BLK), BF),
            pltpu.VMEM((NW, NW), BF),
            pltpu.VMEM((steps, 2, 4, CR, NW), F32),
            pltpu.VMEM((steps, 2, 4, CR, NW), BF),
            pltpu.VMEM((steps, 2, 4, CR, NW), BF),
            pltpu.VMEM((steps, 2, 4, CR, NW), BF),
            pltpu.VMEM((steps, 3, 2, CR, NW), BF),
            pltpu.VMEM((steps, 2, CR, NW), F32),
            pltpu.VMEM((steps, 2, CR, NW), BF),
            pltpu.VMEM((CH, 3, CR, NW), BF),
            pltpu.VMEM((rows, NW), F32),
            pltpu.VMEM((2, BLK, NW), BF),
            pltpu.VMEM((2, BLK, NW), BF),
            dma((CH,)), dma((NB,)),
            dma((CH, 3)), dma((CH, 3)),
            dma((steps,)), dma((steps,)),
            dma((steps, 3)), dma((steps, 3)),
            dma((CH, 3)), dma((CH, 3)),
            dma((2,)), dma((2,)), dma,
        ],
        compiler_params=pltpu.CompilerParams(
            collective_id=0, has_side_effects=True, vmem_limit_bytes=52 * 2**20
        ),
        name="ladder",
    )(
        tiles, integral, tile_mask.transpose(1, 2, 0), pair_irrep,
        slice_irrep.reshape(1, -1), integral_mask,
    )
    return result.reshape(rows_i, rows_j, NW)


def solution(mesh):
    placed = (
        P("occi", "occj", None, "virt"),
        P("occi", "virt", None),
        P("occi", None, "virt"),
        P("occi", "virt"),
        P(),
        P("occi", "virt", None),
    )
    return jax.shard_map(
        shards, mesh=mesh, in_specs=placed, out_specs=P("occi", "occj", "virt"), check_vma=False
    )
```

```python
import jax
import jax.numpy as jnp
from jax import lax
from jax.experimental import pallas as pl
from jax.experimental.pallas import tpu as pltpu
from jax.sharding import PartitionSpec as P

MESH = pl.DeviceIdType.MESH
BF = jnp.bfloat16
F32 = jnp.float32
ROWS = 200
SIZES = (16, 64, 64, 40, 16)
HALVES = (1, 1, 1, 1, 2)
STARTS = tuple(sum(SIZES[:k]) for k in range(len(SIZES)))
CHUNKS = range(len(SIZES))
GROUPS = ((), (0, 1), (2,), (3,), (4,))
LAST = len(GROUPS) - 1
BL = 16
VB = 128
W = BL * VB
NB = 8
NW = 256
TR = 208
TB = 112
TCUT = 96
PIECES = ((0, 0, TB), (1, TCUT, 48), (1, 144, 64))


def group_rows(g):
    return ROWS if g == 0 else sum(SIZES[k] for k in GROUPS[g])


def iota(shape, axis):
    return lax.broadcasted_iota(jnp.int32, shape, axis)


def matmul(a, b):
    return jnp.dot(a, b, preferred_element_type=F32)


def bits(condition):
    return jnp.where(condition, 1.0, 0.0).astype(BF)


def tenth(x):
    return lax.shift_right_logical(x * 205, 11)


def scratch():
    dma = pltpu.SemaphoreType.DMA
    out = dict(
        tm=pltpu.VMEM((4, BL, 20), jnp.int32),
        pi=pltpu.VMEM((1, BL), jnp.int32),
        si=pltpu.VMEM((1, BL), jnp.int32),
        im=pltpu.VMEM((1, BL, BL), jnp.int32),
        v=pltpu.VMEM((NB, W, NW), BF),
        kx=pltpu.VMEM((NB, BL, NW), F32),
        expand=pltpu.VMEM((BL, W), BF),
        turn=pltpu.VMEM((ROWS, 2 * TB), BF),
        swap=pltpu.VMEM((NW, NW), BF),
        total=pltpu.VMEM((ROWS, NW), F32),
        final=pltpu.VMEM((NW // VB, ROWS, VB), F32),
        ts=pltpu.VMEM((TR, NW), BF),
        tr=pltpu.VMEM((2, TR, NW), BF),
        small_sem=dma((4,)), v_sem=dma((NB,)),
        t_ss=dma((3,)), t_rs=dma((3, 2)), t_ls=dma((3,)),
        part=pltpu.VMEM((NB, 2 * SIZES[-1], NW), F32),
        ds=pltpu.VMEM((2, 2, 4, SIZES[-1], NW), BF),
        dr=pltpu.VMEM((2, 2, 4, SIZES[-1], NW), BF),
        d_ss=dma((2, 2, 4)), d_rs=dma((2, 2, 4)),
    )
    for k in CHUNKS:
        r = SIZES[k]
        out.update({
            f"raw{k}": pltpu.VMEM((BL, r, 4, VB), BF),
            f"ma{k}": pltpu.VMEM((4, HALVES[k], r, W // HALVES[k]), BF),
            f"got{k}": pltpu.VMEM((3, HALVES[k], r, W // HALVES[k]), BF),
            f"raw_sem{k}": dma, f"a_ss{k}": dma((3, 2)), f"a_rs{k}": dma((3, 2)),
        })
    for g in range(LAST + 1):
        r = group_rows(g)
        out[f"lhs{g}"] = pltpu.VMEM((2 * r, W), BF)
        if g == LAST:
            break
        out.update({
            f"pk{g}": pltpu.VMEM((2, 4, r, NW), F32),
            f"cs{g}": pltpu.VMEM((2, 4, r, NW), BF),
            f"cr{g}": pltpu.VMEM((2, 4, r, NW), BF),
            f"ys{g}": pltpu.VMEM((2, 4, r, NW), BF),
            f"yr{g}": pltpu.VMEM((3, 2, r, NW), BF),
            f"xt{g}": pltpu.VMEM((2, r, NW), F32),
            f"xs{g}": pltpu.VMEM((2, r, NW), BF),
            f"xr{g}": pltpu.VMEM((2, r, NW), BF),
            f"c_ss{g}": dma, f"c_rs{g}": dma,
            f"y_ss{g}": dma((3,)), f"y_rs{g}": dma((3,)),
            f"x_ss{g}": dma((2,)), f"x_rs{g}": dma((2,)),
        })
    return out


SCRATCH = scratch()


def kernel(amp, vint, tm_in, pi_in, si_in, im_in, out, *refs):
    m = dict(zip(SCRATCH, refs))
    occi, z, virt = lax.axis_index("occi"), lax.axis_index("occj"), lax.axis_index("virt")
    xh, c = occi // 2, occi % 2
    xl, y = virt // 4, virt % 4

    def dev(h, core, low, yy):
        return (2 * h + core, z, 4 * low + yy)

    sibling = dev(xh, 1 - c, xl, y)
    far_same = dev(1 - xh, c, xl, y)
    far_other = dev(1 - xh, 1 - c, xl, y)
    near = dev(xh, c, 1 - xl, y)
    far_near = dev(1 - xh, c, 1 - xl, y)
    y_peer = [dev(xh, c, xl, (y + d) % 4) for d in (1, 2, 3)]
    turned = [(z // 2, 2 * occi + h, virt) for h in (0, 1)]
    on_diag = (z // 2) == occi
    here = z % 2

    def remote(src, dst, send, recv, peer):
        return pltpu.make_async_remote_copy(
            src_ref=src, dst_ref=dst, send_sem=send, recv_sem=recv,
            device_id=peer, device_id_type=MESH,
        )

    smalls = [
        (ref, m[name], m["small_sem"].at[n])
        for n, (ref, name) in enumerate(
            ((tm_in, "tm"), (pi_in, "pi"), (si_in, "si"), (im_in, "im"))
        )
    ]

    def start_raw(k):
        def start(t, _):
            pltpu.make_async_copy(
                amp.at[pl.ds(STARTS[k], SIZES[k]), t], m[f"raw{k}"].at[t], m[f"raw_sem{k}"]
            ).start()
            return 0

        lax.fori_loop(0, BL, start, 0)

    def v_copy(n):
        return pltpu.make_async_copy(
            vint.at[0, :, pl.ds(pl.multiple_of(n * NW, NW), NW)], m["v"].at[n], m["v_sem"].at[n]
        )

    def start_v(n, _):
        v_copy(n).start()
        return 0

    pltpu.make_async_copy(*smalls[0]).start()
    start_raw(0)

    barrier = pltpu.get_barrier_semaphore()
    far = [dev(1 - xh, core, low, yy) for core in (0, 1) for low in (0, 1) for yy in range(4)]
    for peer in far + [sibling, near] + y_peer:
        pl.semaphore_signal(barrier, inc=1, device_id=peer, device_id_type=MESH)
    for h in (0, 1):
        @pl.when(jnp.logical_not(jnp.logical_and(on_diag, here == h)))
        def _():
            pl.semaphore_signal(barrier, inc=1, device_id=turned[h], device_id_type=MESH)

    start_raw(1)
    for args in smalls[1:]:
        pltpu.make_async_copy(*args).start()

    expand = m["expand"]
    expand[...] = bits(lax.shift_right_logical(iota((BL, W), 1), 7) == iota((BL, W), 0))
    pltpu.make_async_copy(*smalls[0]).wait()
    marks = [m["tm"][q].astype(F32).astype(BF) for q in range(4)]

    def a_copies(k):
        far_q = 2 * (1 - xh)
        plan = ((far_q + c, far_same), (far_q + 1 - c, far_other), (2 * xh + 1 - c, sibling))
        return [
            [
                remote(
                    m[f"ma{k}"].at[q, cut], m[f"got{k}"].at[n, cut],
                    m[f"a_ss{k}"].at[n, cut], m[f"a_rs{k}"].at[n, cut], peer,
                )
                for cut in range(HALVES[k])
            ]
            for n, (q, peer) in enumerate(plan)
        ]

    def spread(k):
        r, ma = SIZES[k], m[f"ma{k}"]
        order = jnp.concatenate(
            [bits(iota((r, 4 * r), 1) == 4 * iota((r, 4 * r), 0) + q) for q in range(4)], axis=0
        )
        gap = iota((r, 20), 0) + STARTS[k] - 10 * iota((r, 20), 1)
        own_i = bits(jnp.logical_and(gap >= 0, gap < 10))
        flags = jnp.concatenate(
            [
                lax.dot_general(own_i, mark, (((1,), (1,)), ((), ())), preferred_element_type=F32)
                for mark in marks
            ],
            axis=0,
        ).astype(BF)
        pltpu.make_async_copy(m[f"raw{k}"], m[f"raw{k}"], m[f"raw_sem{k}"]).wait()
        flat = m[f"raw{k}"].reshape(BL, 4 * r, VB)

        per_cut = 4 // HALVES[k]

        def part(p, _):
            x = jnp.concatenate([flat[p * 4 + t] for t in range(4)], axis=1)
            lanes = pl.ds(pl.multiple_of(p * 4 * VB, 4 * VB), 4 * VB)
            got = matmul(order, x) * matmul(flags, expand[:, lanes])
            into = pl.ds(pl.multiple_of(p % per_cut * 4 * VB, 4 * VB), 4 * VB)
            for q in range(4):
                ma[q, p // per_cut, :, into] = got[q * r:(q + 1) * r].astype(BF)
            return 0

        lax.fori_loop(0, 4, part, 0, unroll=4 if k == 0 else 1)

    for k in CHUNKS:
        spread(k)
        if k == 0:
            pl.semaphore_wait(barrier, 23 - on_diag.astype(jnp.int32))
        plan = a_copies(k)
        for cut in range(HALVES[k]):
            for n in range(3):
                plan[n][cut].start()
        if k + 2 in CHUNKS:
            start_raw(k + 2)
        if k == 1:
            lax.fori_loop(0, NB, start_v, 0)

    v = m["v"]
    for args in smalls[1:]:
        pltpu.make_async_copy(*args).wait()
    eye = iota((BL, BL), 0) == iota((BL, BL), 1)
    own_label = jnp.sum(jnp.where(eye, m["pi"][...], 0), axis=1, keepdims=True)
    keep = jnp.where(own_label == m["si"][...], m["im"][0], 0).astype(F32).astype(BF)
    for n in range(NB):
        m["kx"][n] = matmul(keep, expand[:, n * NW:(n + 1) * NW])

    def mask_v(n, _):
        v_copy(n).wait()
        for b in range(BL):
            line = jnp.broadcast_to(m["kx"][n, b:b + 1, :], (16, NW)).astype(BF)
            rows = pl.ds(b * VB, VB)
            v[n, rows, :] = (v[n, rows, :].reshape(8, 16, NW) * line[None]).reshape(VB, NW)
        return 0

    lax.fori_loop(0, NB, mask_v, 0)

    def c_copy(g):
        return remote(m[f"cs{g}"], m[f"cr{g}"], m[f"c_ss{g}"], m[f"c_rs{g}"], sibling)

    def y_copies(g):
        return [
            remote(
                m[f"ys{g}"].at[:, (y + d) % 4], m[f"yr{g}"].at[d - 1],
                m[f"y_ss{g}"].at[d - 1], m[f"y_rs{g}"].at[d - 1], y_peer[d - 1],
            )
            for d in (1, 2, 3)
        ]

    def x_copies(g):
        plan = ((1 - xl, near),) if g == 0 else ((xl, far_same), (1 - xl, far_near))
        return [
            remote(
                m[f"xs{g}"].at[low], m[f"xr{g}"].at[n],
                m[f"x_ss{g}"].at[n], m[f"x_rs{g}"].at[n], peer,
            )
            for n, (low, peer) in enumerate(plan)
        ]

    def stack(pieces):
        if all(piece.shape[0] % 16 == 0 for piece in pieces):
            return jnp.concatenate(pieces, axis=0)
        return jnp.concatenate([p.astype(F32) for p in pieces], axis=0).astype(BF)

    def multiply(g):
        lhs, r = m[f"lhs{g}"], group_rows(g)
        if g == 0:
            pieces = []
            for k in CHUNKS:
                for copy in a_copies(k)[2]:
                    copy.wait_recv()
            for name, slot in (("ma", 2 * xh + c), ("got", 2)):
                for k in CHUNKS:
                    cuts = [m[f"{name}{k}"][slot, cut] for cut in range(HALVES[k])]
                    pieces.append(jnp.concatenate(cuts, axis=1))
            lhs[...] = stack(pieces)
        else:
            for k in GROUPS[g]:
                for n in range(2):
                    a_copies(k)[n][0].wait_recv()
            pieces = [m[f"got{k}"][n, 0] for n in range(2) for k in GROUPS[g]]
            lhs[:, :pieces[0].shape[1]] = stack(pieces)

        def column(n, _):
            got = matmul(lhs[...], v[n])
            m[f"pk{g}"][n // 4, n % 4] = got[:r]
            m[f"cs{g}"][n // 4, n % 4] = got[r:].astype(BF)
            return 0

        half = W // 2

        def first_half(n, _):
            m["part"][n] = matmul(lhs[:, :half], v[n, :half, :])
            return 0

        def second_half(n, _):
            got = m["part"][n] + matmul(lhs[:, half:], v[n, half:, :])
            for a in range(2):
                m["ds"][a, n // 4, n % 4] = got[a * r:(a + 1) * r].astype(BF)
            return 0

        if g == LAST:
            lax.fori_loop(0, NB, first_half, 0, unroll=2)
            last = GROUPS[g][0]
            for n in range(2):
                a_copies(last)[n][1].wait_recv()
            lhs[:, half:] = stack([m[f"got{last}"][n, 1] for n in range(2)])
            lax.fori_loop(0, NB, second_half, 0, unroll=2)
        else:
            lax.fori_loop(0, NB, column, 0, unroll=1 if g == 0 else 2)
        for copy in direct() if g == LAST else [c_copy(g)]:
            copy.start()

    def over_cores(g):
        pk, cr, ys = m[f"pk{g}"], m[f"cr{g}"], m[f"ys{g}"]
        c_copy(g).wait_recv()
        for low in range(2):
            for yy in range(4):
                both = pk[low, yy] + cr[low, yy].astype(F32)
                pk[low, yy] = both
                ys[low, yy] = both.astype(BF)
        for copy in y_copies(g):
            copy.start()

    def over_y(g):
        pk, yr, xt, xs = m[f"pk{g}"], m[f"yr{g}"], m[f"xt{g}"], m[f"xs{g}"]
        for copy in y_copies(g):
            copy.wait_recv()
        for low in range(2):
            both = pk[low, y]
            for d in range(3):
                both = both + yr[d, low].astype(F32)
            xt[low] = both
            xs[low] = both.astype(BF)
        for copy in x_copies(g):
            copy.start()

    def direct():
        return [
            remote(
                m["ds"].at[a, (xl + b) % 2, (y + d) % 4], m["dr"].at[a, b, d],
                m["d_ss"].at[a, b, d], m["d_rs"].at[a, b, d],
                dev(1 - xh, (c + a) % 2, (xl + b) % 2, (y + d) % 4),
            )
            for a in range(2) for b in range(2) for d in range(4)
        ]

    total = m["total"]

    def over_x(g):
        if g == 0:
            x_copies(g)[0].wait_recv()
            total[...] = m["xt0"][xl] + m["xr0"][0].astype(F32)
            return
        first = STARTS[GROUPS[g][0]]
        rows = slice(first, first + group_rows(g))
        if g == LAST:
            for copy in direct():
                copy.wait_recv()
            terms = [m["dr"][a, b, d] for a in range(2) for b in range(2) for d in range(4)]
        else:
            for copy in x_copies(g):
                copy.wait_recv()
            terms = [m[f"xr{g}"][n] for n in range(2)]
        both = total[rows]
        for term in terms:
            both = both + term.astype(F32)
        total[rows] = both

    ts, tr = m["ts"], m["tr"]

    def t_copy(p, slot):
        h, first, rows = PIECES[p]
        return remote(
            ts.at[pl.ds(first, rows)], tr.at[slot, pl.ds(first, rows)],
            m["t_ss"].at[p], m["t_rs"].at[p, slot], turned[h],
        )

    def t_local(p):
        h, first, rows = PIECES[p]
        return pltpu.make_async_copy(
            ts.at[pl.ds(first, rows)], tr.at[h, pl.ds(first, rows)], m["t_ls"].at[p]
        )

    def t_mine(p):
        return jnp.logical_and(on_diag, here == PIECES[p][0])

    def mirror(first, rows):
        some = matmul(total[first:first + rows].astype(BF), m["swap"][...]).astype(BF)
        ts[first:first + rows, :] = some

    def t_start(p):
        @pl.when(t_mine(p))
        def _():
            t_local(p).start()

        @pl.when(jnp.logical_not(t_mine(p)))
        def _():
            t_copy(p, here).start()

    def t_wait(p):
        block = PIECES[p][0]

        @pl.when(t_mine(p))
        def _():
            t_local(p).wait()

        @pl.when(jnp.logical_not(t_mine(p)))
        def _():
            t_copy(p, here).wait_send()

        for slot in (0, 1):
            there = jnp.logical_not(jnp.logical_and(on_diag, here == slot))

            @pl.when(jnp.logical_and(here == block, there))
            def _():
                t_copy(p, slot).wait_recv()

    def matrices():
        rt, ct = iota((ROWS, 2 * TB), 0), iota((ROWS, 2 * TB), 1)
        it = tenth(rt)
        jt = rt - 10 * it
        ht = jnp.where(it >= 10, 1, 0)
        m["turn"][...] = bits(ct == TB * ht + 4 * here + jt * 10 + it - 10 * ht)
        aw, bw = iota((NW, NW), 0), iota((NW, NW), 1)
        m["swap"][...] = bits(aw == bw + 1 - 2 * jnp.bitwise_and(bw, 1))
        ts[ROWS - 8:TR, :] = jnp.zeros((16, NW), BF)

    multiply(0)
    matrices()
    over_cores(0)
    multiply(1)
    over_cores(1)
    over_y(0)
    multiply(2)
    over_y(1)
    over_cores(2)
    multiply(3)
    over_cores(3)
    over_y(2)
    multiply(4)
    over_y(3)
    over_x(0)
    over_x(1)
    over_x(2)
    mirror(0, 144)
    t_start(0)
    t_start(1)
    over_x(3)
    over_x(4)
    mirror(144, 56)
    t_start(2)

    for k in CHUNKS:
        for copies in a_copies(k):
            for copy in copies:
                copy.wait_send()
    for g in range(LAST):
        for copy in [c_copy(g)] + y_copies(g) + x_copies(g):
            copy.wait_send()
    for copy in direct():
        copy.wait_send()
    for p in range(len(PIECES)):
        t_wait(p)

    rows = pl.ds(pl.multiple_of(TCUT * here, 16), TB)
    arrived = jnp.concatenate([tr[0, rows, :], tr[1, rows, :]], axis=0)
    both = total[...] + matmul(m["turn"][...], arrived)
    for n in range(NW // VB):
        lanes = slice(n * VB, (n + 1) * VB)
        m["final"][n] = both[:, lanes]
        for j in range(10):
            out[j, :, lanes] = m["final"][n, pl.ds(j, 20, stride=10), :].astype(BF)


def shards(amplitude, integral, tile_mask, pair_irrep, slice_irrep, integral_mask):
    rows_i, rows_j, groups, _ = amplitude.shape
    tiles = amplitude.reshape(ROWS, groups, BL, VB).transpose(0, 2, 1, 3)
    hbm = pl.BlockSpec(memory_space=pltpu.HBM)
    result = pl.pallas_call(
        kernel,
        out_shape=jax.ShapeDtypeStruct((rows_j, rows_i, NW), BF),
        in_specs=[hbm] * 6,
        out_specs=pl.BlockSpec(memory_space=pltpu.VMEM),
        scratch_shapes=list(SCRATCH.values()),
        compiler_params=pltpu.CompilerParams(
            collective_id=0, has_side_effects=True, vmem_limit_bytes=56 * 2**20
        ),
        name="ladder",
    )(
        tiles, integral, tile_mask.transpose(1, 2, 0), pair_irrep,
        slice_irrep.reshape(1, -1), integral_mask,
    )
    return result.transpose(1, 0, 2)


def solution(mesh):
    placed = (
        P("occi", "occj", None, "virt"),
        P("occi", "virt", None),
        P("occi", None, "virt"),
        P("occi", "virt"),
        P(),
        P("occi", "virt", None),
    )
    return jax.shard_map(
        shards, mesh=mesh, in_specs=placed, out_specs=P("occi", "occj", "virt"), check_vma=False
    )
```

```python
import jax
import jax.numpy as jnp
from jax import lax
from jax.experimental import pallas as pl
from jax.experimental.pallas import tpu as pltpu
from jax.sharding import PartitionSpec as P

MESH = pl.DeviceIdType.MESH
BF = jnp.bfloat16
F32 = jnp.float32
ROWS = 200
SIZES = (16, 64, 64, 40, 16)
HALVES = (1, 1, 1, 1, 2)
STARTS = tuple(sum(SIZES[:k]) for k in range(len(SIZES)))
CHUNKS = range(len(SIZES))
GROUPS = ((), (0, 1), (2,), (3,), (4,))
DIRECT = (3, 4)
BL = 16
VB = 128
W = BL * VB
NB = 8
NW = 256
TR = 208
TB = 112
TCUT = 96
PIECES = ((0, 0, TB), (1, TCUT, 48), (1, 144, 64))
FROM_BOTH = tuple(k for g in DIRECT for k in GROUPS[g])


def group_rows(g):
    return ROWS if g == 0 else sum(SIZES[k] for k in GROUPS[g])


def iota(shape, axis):
    return lax.broadcasted_iota(jnp.int32, shape, axis)


def matmul(a, b):
    return jnp.dot(a, b, preferred_element_type=F32)


def bits(condition):
    return jnp.where(condition, 1.0, 0.0).astype(BF)


def tenth(x):
    return lax.shift_right_logical(x * 205, 11)


def scratch():
    dma = pltpu.SemaphoreType.DMA
    out = dict(
        tm=pltpu.VMEM((4, BL, 20), jnp.int32),
        pi=pltpu.VMEM((1, BL), jnp.int32),
        si=pltpu.VMEM((1, BL), jnp.int32),
        im=pltpu.VMEM((1, BL, BL), jnp.int32),
        v=pltpu.VMEM((NB, W, NW), BF),
        kx=pltpu.VMEM((NB, BL, NW), F32),
        expand=pltpu.VMEM((BL, W), BF),
        turn=pltpu.VMEM((ROWS, 2 * TB), BF),
        swap=pltpu.VMEM((NW, NW), BF),
        total=pltpu.VMEM((ROWS, NW), F32),
        final=pltpu.VMEM((NW // VB, ROWS, VB), F32),
        ts=pltpu.VMEM((TR, NW), BF),
        tr=pltpu.VMEM((2, TR, NW), BF),
        small_sem=dma((4,)), v_sem=dma((NB,)),
        t_ss=dma((3,)), t_rs=dma((3, 2)), t_ls=dma((3,)),
        vs=pltpu.VMEM((NB, W, NW), BF),
        vs_ss=dma((NB,)), vs_rs=dma((NB,)),
    )
    for k in CHUNKS:
        r = SIZES[k]
        out.update({
            f"raw{k}": pltpu.VMEM((BL, r, 4, VB), BF),
            f"ma{k}": pltpu.VMEM((4, HALVES[k], r, W // HALVES[k]), BF),
            f"got{k}": pltpu.VMEM((3, HALVES[k], r, W // HALVES[k]), BF),
            f"raw_sem{k}": dma, f"a_ss{k}": dma((3, 2)), f"a_rs{k}": dma((3, 2)),
        })
    for g in range(len(GROUPS)):
        r = group_rows(g)
        if g in DIRECT:
            out.update({
                f"part{g}": pltpu.VMEM((NB, r, NW), F32),
                f"ds{g}": pltpu.VMEM((2, 4, r, NW), BF),
                f"dr{g}": pltpu.VMEM((2, 4, r, NW), BF),
                f"d_ss{g}": dma((2, 4)), f"d_rs{g}": dma((2, 4)),
            })
            continue
        out.update({
            f"lhs{g}": pltpu.VMEM((2 * r, W), BF),
            f"pk{g}": pltpu.VMEM((2, 4, r, NW), F32),
            f"cs{g}": pltpu.VMEM((2, 4, r, NW), BF),
            f"cr{g}": pltpu.VMEM((2, 4, r, NW), BF),
            f"ys{g}": pltpu.VMEM((2, 4, r, NW), BF),
            f"yr{g}": pltpu.VMEM((3, 2, r, NW), BF),
            f"xt{g}": pltpu.VMEM((2, r, NW), F32),
            f"xs{g}": pltpu.VMEM((2, r, NW), BF),
            f"xr{g}": pltpu.VMEM((2, r, NW), BF),
            f"c_ss{g}": dma, f"c_rs{g}": dma,
            f"y_ss{g}": dma((3,)), f"y_rs{g}": dma((3,)),
            f"x_ss{g}": dma((2,)), f"x_rs{g}": dma((2,)),
        })
    return out


SCRATCH = scratch()


def kernel(amp, vint, tm_in, pi_in, si_in, im_in, out, *refs):
    m = dict(zip(SCRATCH, refs))
    occi, z, virt = lax.axis_index("occi"), lax.axis_index("occj"), lax.axis_index("virt")
    xh, c = occi // 2, occi % 2
    xl, y = virt // 4, virt % 4

    def dev(h, core, low, yy):
        return (2 * h + core, z, 4 * low + yy)

    sibling = dev(xh, 1 - c, xl, y)
    far_same = dev(1 - xh, c, xl, y)
    far_other = dev(1 - xh, 1 - c, xl, y)
    near = dev(xh, c, 1 - xl, y)
    far_near = dev(1 - xh, c, 1 - xl, y)
    y_peer = [dev(xh, c, xl, (y + d) % 4) for d in (1, 2, 3)]
    turned = [(z // 2, 2 * occi + h, virt) for h in (0, 1)]
    on_diag = (z // 2) == occi
    here = z % 2

    def remote(src, dst, send, recv, peer):
        return pltpu.make_async_remote_copy(
            src_ref=src, dst_ref=dst, send_sem=send, recv_sem=recv,
            device_id=peer, device_id_type=MESH,
        )

    smalls = [
        (ref, m[name], m["small_sem"].at[n])
        for n, (ref, name) in enumerate(
            ((tm_in, "tm"), (pi_in, "pi"), (si_in, "si"), (im_in, "im"))
        )
    ]

    def start_raw(k):
        def start(t, _):
            pltpu.make_async_copy(
                amp.at[pl.ds(STARTS[k], SIZES[k]), t], m[f"raw{k}"].at[t], m[f"raw_sem{k}"]
            ).start()
            return 0

        lax.fori_loop(0, BL, start, 0)

    def v_copy(n):
        return pltpu.make_async_copy(
            vint.at[0, :, pl.ds(pl.multiple_of(n * NW, NW), NW)], m["v"].at[n], m["v_sem"].at[n]
        )

    def start_v(n, _):
        v_copy(n).start()
        return 0

    pltpu.make_async_copy(*smalls[0]).start()
    start_raw(0)

    barrier = pltpu.get_barrier_semaphore()
    far = [dev(1 - xh, c, low, yy) for low in (0, 1) for yy in range(4)]
    for peer in far + [far_other, sibling, near] + y_peer:
        pl.semaphore_signal(barrier, inc=1, device_id=peer, device_id_type=MESH)
    for h in (0, 1):
        @pl.when(jnp.logical_not(jnp.logical_and(on_diag, here == h)))
        def _():
            pl.semaphore_signal(barrier, inc=1, device_id=turned[h], device_id_type=MESH)

    start_raw(1)
    for args in smalls[1:]:
        pltpu.make_async_copy(*args).start()

    expand = m["expand"]
    expand[...] = bits(lax.shift_right_logical(iota((BL, W), 1), 7) == iota((BL, W), 0))
    pltpu.make_async_copy(*smalls[0]).wait()
    marks = [m["tm"][q].astype(F32).astype(BF) for q in range(4)]

    def a_copies(k):
        far_q = 2 * (1 - xh)
        second = far_same if k in FROM_BOTH else far_other
        plan = ((far_q + c, far_same), (far_q + 1 - c, second), (2 * xh + 1 - c, sibling))
        return [
            [
                remote(
                    m[f"ma{k}"].at[q, cut], m[f"got{k}"].at[n, cut],
                    m[f"a_ss{k}"].at[n, cut], m[f"a_rs{k}"].at[n, cut], peer,
                )
                for cut in range(HALVES[k])
            ]
            for n, (q, peer) in enumerate(plan)
        ]

    def spread(k):
        r, ma = SIZES[k], m[f"ma{k}"]
        order = jnp.concatenate(
            [bits(iota((r, 4 * r), 1) == 4 * iota((r, 4 * r), 0) + q) for q in range(4)], axis=0
        )
        gap = iota((r, 20), 0) + STARTS[k] - 10 * iota((r, 20), 1)
        own_i = bits(jnp.logical_and(gap >= 0, gap < 10))
        flags = jnp.concatenate(
            [
                lax.dot_general(own_i, mark, (((1,), (1,)), ((), ())), preferred_element_type=F32)
                for mark in marks
            ],
            axis=0,
        ).astype(BF)
        pltpu.make_async_copy(m[f"raw{k}"], m[f"raw{k}"], m[f"raw_sem{k}"]).wait()
        flat = m[f"raw{k}"].reshape(BL, 4 * r, VB)

        per_cut = 4 // HALVES[k]

        def part(p, _):
            x = jnp.concatenate([flat[p * 4 + t] for t in range(4)], axis=1)
            lanes = pl.ds(pl.multiple_of(p * 4 * VB, 4 * VB), 4 * VB)
            got = matmul(order, x) * matmul(flags, expand[:, lanes])
            into = pl.ds(pl.multiple_of(p % per_cut * 4 * VB, 4 * VB), 4 * VB)
            for q in range(4):
                ma[q, p // per_cut, :, into] = got[q * r:(q + 1) * r].astype(BF)
            return 0

        lax.fori_loop(0, 4, part, 0, unroll=4 if k == 0 else 1)

    for k in CHUNKS:
        spread(k)
        if k == 0:
            pl.semaphore_wait(barrier, 16 - on_diag.astype(jnp.int32))
        plan = a_copies(k)
        for cut in range(HALVES[k]):
            for n in range(3):
                plan[n][cut].start()
        if k + 2 in CHUNKS:
            start_raw(k + 2)
        if k == 1:
            lax.fori_loop(0, NB, start_v, 0)

    v = m["v"]
    for args in smalls[1:]:
        pltpu.make_async_copy(*args).wait()
    eye = iota((BL, BL), 0) == iota((BL, BL), 1)
    own_label = jnp.sum(jnp.where(eye, m["pi"][...], 0), axis=1, keepdims=True)
    keep = jnp.where(own_label == m["si"][...], m["im"][0], 0).astype(F32).astype(BF)
    for n in range(NB):
        m["kx"][n] = matmul(keep, expand[:, n * NW:(n + 1) * NW])

    def mask_v(n, _):
        v_copy(n).wait()
        for b in range(BL):
            line = jnp.broadcast_to(m["kx"][n, b:b + 1, :], (16, NW)).astype(BF)
            rows = pl.ds(b * VB, VB)
            v[n, rows, :] = (v[n, rows, :].reshape(8, 16, NW) * line[None]).reshape(VB, NW)
        return 0

    lax.fori_loop(0, NB, mask_v, 0)

    def c_copy(g):
        return remote(m[f"cs{g}"], m[f"cr{g}"], m[f"c_ss{g}"], m[f"c_rs{g}"], sibling)

    def y_copies(g):
        return [
            remote(
                m[f"ys{g}"].at[:, (y + d) % 4], m[f"yr{g}"].at[d - 1],
                m[f"y_ss{g}"].at[d - 1], m[f"y_rs{g}"].at[d - 1], y_peer[d - 1],
            )
            for d in (1, 2, 3)
        ]

    def x_copies(g):
        plan = ((1 - xl, near),) if g == 0 else ((xl, far_same), (1 - xl, far_near))
        return [
            remote(
                m[f"xs{g}"].at[low], m[f"xr{g}"].at[n],
                m[f"x_ss{g}"].at[n], m[f"x_rs{g}"].at[n], peer,
            )
            for n, (low, peer) in enumerate(plan)
        ]

    def stack(pieces):
        if all(piece.shape[0] % 16 == 0 for piece in pieces):
            return jnp.concatenate(pieces, axis=0)
        return jnp.concatenate([p.astype(F32) for p in pieces], axis=0).astype(BF)

    def multiply(g):
        lhs, r = m[f"lhs{g}"], group_rows(g)
        if g == 0:
            pieces = []
            for k in CHUNKS:
                for copy in a_copies(k)[2]:
                    copy.wait_recv()
            for name, slot in (("ma", 2 * xh + c), ("got", 2)):
                for k in CHUNKS:
                    cuts = [m[f"{name}{k}"][slot, cut] for cut in range(HALVES[k])]
                    pieces.append(jnp.concatenate(cuts, axis=1))
            lhs[...] = stack(pieces)
        else:
            for k in GROUPS[g]:
                for n in range(2):
                    a_copies(k)[n][0].wait_recv()
            pieces = [m[f"got{k}"][n, 0] for n in range(2) for k in GROUPS[g]]
            lhs[:, :pieces[0].shape[1]] = stack(pieces)

        def column(n, _):
            got = matmul(lhs[...], v[n])
            m[f"pk{g}"][n // 4, n % 4] = got[:r]
            m[f"cs{g}"][n // 4, n % 4] = got[r:].astype(BF)
            return 0

        lax.fori_loop(0, NB, column, 0, unroll=1 if g == 0 else 2)
        c_copy(g).start()

    def vs_copy(n):
        return remote(v.at[n], m["vs"].at[n], m["vs_ss"].at[n], m["vs_rs"].at[n], sibling)

    def share_v(first):
        def start(n, _):
            vs_copy(first + n).start()
            return 0

        lax.fori_loop(0, NB // 2, start, 0)

    def wait_v():
        def wait(n, _):
            vs_copy(n).wait_recv()
            return 0

        lax.fori_loop(0, NB, wait, 0)

    def d_copies(g):
        return [
            remote(
                m[f"ds{g}"].at[(xl + b) % 2, (y + d) % 4], m[f"dr{g}"].at[b, d],
                m[f"d_ss{g}"].at[b, d], m[f"d_rs{g}"].at[b, d],
                dev(1 - xh, c, (xl + b) % 2, (y + d) % 4),
            )
            for b in range(2) for d in range(4)
        ]

    def multiply_whole(g):
        k = GROUPS[g][0]
        part, depth = m[f"part{g}"], W // HALVES[k]
        steps = [(cut, n) for cut in range(HALVES[k]) for n in range(2)]
        for at, (cut, n) in enumerate(steps):
            a_copies(k)[n][cut].wait_recv()
            weights = v if n == 0 else m["vs"]

            def column(b, _):
                got = matmul(m[f"got{k}"][n, cut], weights[b, cut * depth:(cut + 1) * depth, :])
                if at > 0:
                    got = got + part[b]
                if at < len(steps) - 1:
                    part[b] = got
                else:
                    m[f"ds{g}"][b // 4, b % 4] = got.astype(BF)
                return 0

            lax.fori_loop(0, NB, column, 0, unroll=2)
        for copy in d_copies(g):
            copy.start()

    def over_cores(g):
        pk, cr, ys = m[f"pk{g}"], m[f"cr{g}"], m[f"ys{g}"]
        c_copy(g).wait_recv()
        for low in range(2):
            for yy in range(4):
                both = pk[low, yy] + cr[low, yy].astype(F32)
                pk[low, yy] = both
                ys[low, yy] = both.astype(BF)
        for copy in y_copies(g):
            copy.start()

    def over_y(g):
        pk, yr, xt, xs = m[f"pk{g}"], m[f"yr{g}"], m[f"xt{g}"], m[f"xs{g}"]
        for copy in y_copies(g):
            copy.wait_recv()
        for low in range(2):
            both = pk[low, y]
            for d in range(3):
                both = both + yr[d, low].astype(F32)
            xt[low] = both
            xs[low] = both.astype(BF)
        for copy in x_copies(g):
            copy.start()

    total = m["total"]

    def over_x(g):
        if g == 0:
            x_copies(g)[0].wait_recv()
            total[...] = m["xt0"][xl] + m["xr0"][0].astype(F32)
            return
        first = STARTS[GROUPS[g][0]]
        rows = slice(first, first + group_rows(g))
        if g in DIRECT:
            for copy in d_copies(g):
                copy.wait_recv()
            terms = [m[f"dr{g}"][b, d] for b in range(2) for d in range(4)]
        else:
            for copy in x_copies(g):
                copy.wait_recv()
            terms = [m[f"xr{g}"][n] for n in range(2)]
        both = total[rows]
        for term in terms:
            both = both + term.astype(F32)
        total[rows] = both

    ts, tr = m["ts"], m["tr"]

    def t_copy(p, slot):
        h, first, rows = PIECES[p]
        return remote(
            ts.at[pl.ds(first, rows)], tr.at[slot, pl.ds(first, rows)],
            m["t_ss"].at[p], m["t_rs"].at[p, slot], turned[h],
        )

    def t_local(p):
        h, first, rows = PIECES[p]
        return pltpu.make_async_copy(
            ts.at[pl.ds(first, rows)], tr.at[h, pl.ds(first, rows)], m["t_ls"].at[p]
        )

    def t_mine(p):
        return jnp.logical_and(on_diag, here == PIECES[p][0])

    def mirror(first, rows):
        some = matmul(total[first:first + rows].astype(BF), m["swap"][...]).astype(BF)
        ts[first:first + rows, :] = some

    def t_start(p):
        @pl.when(t_mine(p))
        def _():
            t_local(p).start()

        @pl.when(jnp.logical_not(t_mine(p)))
        def _():
            t_copy(p, here).start()

    def t_wait(p):
        block = PIECES[p][0]

        @pl.when(t_mine(p))
        def _():
            t_local(p).wait()

        @pl.when(jnp.logical_not(t_mine(p)))
        def _():
            t_copy(p, here).wait_send()

        for slot in (0, 1):
            there = jnp.logical_not(jnp.logical_and(on_diag, here == slot))

            @pl.when(jnp.logical_and(here == block, there))
            def _():
                t_copy(p, slot).wait_recv()

    def matrices():
        rt, ct = iota((ROWS, 2 * TB), 0), iota((ROWS, 2 * TB), 1)
        it = tenth(rt)
        jt = rt - 10 * it
        ht = jnp.where(it >= 10, 1, 0)
        m["turn"][...] = bits(ct == TB * ht + 4 * here + jt * 10 + it - 10 * ht)
        aw, bw = iota((NW, NW), 0), iota((NW, NW), 1)
        m["swap"][...] = bits(aw == bw + 1 - 2 * jnp.bitwise_and(bw, 1))
        ts[ROWS - 8:TR, :] = jnp.zeros((16, NW), BF)

    multiply(0)
    share_v(0)
    matrices()
    over_cores(0)
    multiply(1)
    share_v(NB // 2)
    over_cores(1)
    over_y(0)
    multiply(2)
    over_y(1)
    over_cores(2)
    wait_v()
    multiply_whole(3)
    over_y(2)
    multiply_whole(4)
    over_x(0)
    over_x(1)
    over_x(2)
    mirror(0, 144)
    t_start(0)
    t_start(1)
    over_x(3)
    over_x(4)
    mirror(144, 56)
    t_start(2)

    for k in CHUNKS:
        for copies in a_copies(k):
            for copy in copies:
                copy.wait_send()
    for g in range(len(GROUPS)):
        for copy in d_copies(g) if g in DIRECT else [c_copy(g)] + y_copies(g) + x_copies(g):
            copy.wait_send()
    for n in range(NB):
        vs_copy(n).wait_send()
    for p in range(len(PIECES)):
        t_wait(p)

    rows = pl.ds(pl.multiple_of(TCUT * here, 16), TB)
    arrived = jnp.concatenate([tr[0, rows, :], tr[1, rows, :]], axis=0)
    both = total[...] + matmul(m["turn"][...], arrived)
    for n in range(NW // VB):
        lanes = slice(n * VB, (n + 1) * VB)
        m["final"][n] = both[:, lanes]
        for j in range(10):
            out[j, :, lanes] = m["final"][n, pl.ds(j, 20, stride=10), :].astype(BF)


def shards(amplitude, integral, tile_mask, pair_irrep, slice_irrep, integral_mask):
    rows_i, rows_j, groups, _ = amplitude.shape
    tiles = amplitude.reshape(ROWS, groups, BL, VB).transpose(0, 2, 1, 3)
    hbm = pl.BlockSpec(memory_space=pltpu.HBM)
    result = pl.pallas_call(
        kernel,
        out_shape=jax.ShapeDtypeStruct((rows_j, rows_i, NW), BF),
        in_specs=[hbm] * 6,
        out_specs=pl.BlockSpec(memory_space=pltpu.VMEM),
        scratch_shapes=list(SCRATCH.values()),
        compiler_params=pltpu.CompilerParams(
            collective_id=0, has_side_effects=True, vmem_limit_bytes=56 * 2**20
        ),
        name="ladder",
    )(
        tiles, integral, tile_mask.transpose(1, 2, 0), pair_irrep,
        slice_irrep.reshape(1, -1), integral_mask,
    )
    return result.transpose(1, 0, 2)


def solution(mesh):
    placed = (
        P("occi", "occj", None, "virt"),
        P("occi", "virt", None),
        P("occi", None, "virt"),
        P("occi", "virt"),
        P(),
        P("occi", "virt", None),
    )
    return jax.shard_map(
        shards, mesh=mesh, in_specs=placed, out_specs=P("occi", "occj", "virt"), check_vma=False
    )
```

```python
import jax
import jax.numpy as jnp
from jax import lax
from jax.experimental import pallas as pl
from jax.experimental.pallas import tpu as pltpu
from jax.sharding import PartitionSpec as P

MESH = pl.DeviceIdType.MESH
BF = jnp.bfloat16
F32 = jnp.float32
ROWS = 200
SIZES = (16, 80, 48, 40, 16)
HALVES = (1, 1, 1, 1, 2)
STARTS = tuple(sum(SIZES[:k]) for k in range(len(SIZES)))
CHUNKS = range(len(SIZES))
GROUPS = ((), (0, 1), (2,), (3,), (4,))
DIRECT = (3, 4)
BL = 16
VB = 128
W = BL * VB
NB = 8
NW = 256
TR = 208
TB = 112
TCUT = 96
PIECES = ((0, 0, TB), (1, TCUT, 48), (1, 144, 64))
FROM_BOTH = tuple(k for g in DIRECT for k in GROUPS[g])


def group_rows(g):
    return ROWS if g == 0 else sum(SIZES[k] for k in GROUPS[g])


def iota(shape, axis):
    return lax.broadcasted_iota(jnp.int32, shape, axis)


def matmul(a, b):
    return jnp.dot(a, b, preferred_element_type=F32)


def bits(condition):
    return jnp.where(condition, 1.0, 0.0).astype(BF)


def tenth(x):
    return lax.shift_right_logical(x * 205, 11)


def scratch():
    dma = pltpu.SemaphoreType.DMA
    out = dict(
        v=pltpu.VMEM((NB, W, NW), BF),
        kx=pltpu.VMEM((NB, BL, NW), F32),
        expand=pltpu.VMEM((BL, W), BF),
        turn=pltpu.VMEM((ROWS, 2 * TB), BF),
        total=pltpu.VMEM((ROWS, NW), F32),
        final=pltpu.VMEM((NW // VB, ROWS, VB), F32),
        ts=pltpu.VMEM((TR, NW), BF),
        tr=pltpu.VMEM((2, TR, NW), BF),
        v_sem=dma((NB,)),
        t_ss=dma((3,)), t_rs=dma((3, 2)), t_ls=dma((3,)),
        vs=pltpu.VMEM((NB, W, NW), BF),
        vs_ss=dma((NB,)), vs_rs=dma((NB,)),
    )
    for k in CHUNKS:
        r = SIZES[k]
        out.update({
            f"raw{k}": pltpu.VMEM((BL, r, 4, VB), BF),
            f"ma{k}": pltpu.VMEM((4, HALVES[k], r, W // HALVES[k]), BF),
            f"got{k}": pltpu.VMEM((3, HALVES[k], r, W // HALVES[k]), BF),
            f"raw_sem{k}": dma, f"a_ss{k}": dma((3, 2)), f"a_rs{k}": dma((3, 2)),
        })
    for g in range(len(GROUPS)):
        r = group_rows(g)
        if g in DIRECT:
            out.update({
                f"part{g}": pltpu.VMEM((NB, r, NW), F32),
                f"ds{g}": pltpu.VMEM((2, 4, r, NW), BF),
                f"dr{g}": pltpu.VMEM((2, 4, r, NW), BF),
                f"d_ss{g}": dma((2, 4)), f"d_rs{g}": dma((2, 4)),
            })
            continue
        out.update({
            f"lhs{g}": pltpu.VMEM((2 * r, W), BF),
            f"pk{g}": pltpu.VMEM((2, 4, r, NW), F32),
            f"cs{g}": pltpu.VMEM((2, 4, r, NW), BF),
            f"cr{g}": pltpu.VMEM((2, 4, r, NW), BF),
            f"ys{g}": pltpu.VMEM((2, 4, r, NW), BF),
            f"yr{g}": pltpu.VMEM((3, 2, r, NW), BF),
            f"xt{g}": pltpu.VMEM((2, r, NW), F32),
            f"xs{g}": pltpu.VMEM((2, r, NW), BF),
            f"xr{g}": pltpu.VMEM((2, r, NW), BF),
            f"c_ss{g}": dma, f"c_rs{g}": dma,
            f"y_ss{g}": dma((3,)), f"y_rs{g}": dma((3,)),
            f"x_ss{g}": dma((2,)), f"x_rs{g}": dma((2,)),
        })
    return out


SCRATCH = scratch()


def kernel(amp, vint, tm, keep, out, *refs):
    m = dict(zip(SCRATCH, refs))
    occi, z, virt = lax.axis_index("occi"), lax.axis_index("occj"), lax.axis_index("virt")
    xh, c = occi // 2, occi % 2
    xl, y = virt // 4, virt % 4

    def dev(h, core, low, yy):
        return (2 * h + core, z, 4 * low + yy)

    sibling = dev(xh, 1 - c, xl, y)
    far_same = dev(1 - xh, c, xl, y)
    far_other = dev(1 - xh, 1 - c, xl, y)
    near = dev(xh, c, 1 - xl, y)
    far_near = dev(1 - xh, c, 1 - xl, y)
    y_peer = [dev(xh, c, xl, (y + d) % 4) for d in (1, 2, 3)]
    turned = [(z // 2, 2 * occi + h, virt) for h in (0, 1)]
    on_diag = (z // 2) == occi
    here = z % 2

    def remote(src, dst, send, recv, peer):
        return pltpu.make_async_remote_copy(
            src_ref=src, dst_ref=dst, send_sem=send, recv_sem=recv,
            device_id=peer, device_id_type=MESH,
        )

    def start_raw(k):
        def start(t, _):
            pltpu.make_async_copy(
                amp.at[pl.ds(STARTS[k], SIZES[k]), t], m[f"raw{k}"].at[t], m[f"raw_sem{k}"]
            ).start()
            return 0

        lax.fori_loop(0, BL, start, 0)

    def v_copy(n):
        return pltpu.make_async_copy(
            vint.at[0, :, pl.ds(pl.multiple_of(n * NW, NW), NW)], m["v"].at[n], m["v_sem"].at[n]
        )

    def start_v(n, _):
        v_copy(n).start()
        return 0

    start_raw(0)

    barrier = pltpu.get_barrier_semaphore()
    far = [dev(1 - xh, c, low, yy) for low in (0, 1) for yy in range(4)]
    for peer in far + [far_other, sibling, near] + y_peer:
        pl.semaphore_signal(barrier, inc=1, device_id=peer, device_id_type=MESH)
    for h in (0, 1):
        @pl.when(jnp.logical_not(jnp.logical_and(on_diag, here == h)))
        def _():
            pl.semaphore_signal(barrier, inc=1, device_id=turned[h], device_id_type=MESH)

    start_raw(1)

    expand = m["expand"]
    expand[...] = bits(lax.shift_right_logical(iota((BL, W), 1), 7) == iota((BL, W), 0))
    marks = [tm[q].astype(BF) for q in range(4)]

    def a_copies(k):
        far_q = 2 * (1 - xh)
        second = far_same if k in FROM_BOTH else far_other
        plan = ((far_q + c, far_same), (far_q + 1 - c, second), (2 * xh + 1 - c, sibling))
        return [
            [
                remote(
                    m[f"ma{k}"].at[q, cut], m[f"got{k}"].at[n, cut],
                    m[f"a_ss{k}"].at[n, cut], m[f"a_rs{k}"].at[n, cut], peer,
                )
                for cut in range(HALVES[k])
            ]
            for n, (q, peer) in enumerate(plan)
        ]

    def spread(k):
        r, ma = SIZES[k], m[f"ma{k}"]
        order = jnp.concatenate(
            [bits(iota((r, 4 * r), 1) == 4 * iota((r, 4 * r), 0) + q) for q in range(4)], axis=0
        )
        gap = iota((r, 20), 0) + STARTS[k] - 10 * iota((r, 20), 1)
        own_i = bits(jnp.logical_and(gap >= 0, gap < 10))
        flags = jnp.concatenate(
            [
                lax.dot_general(own_i, mark, (((1,), (1,)), ((), ())), preferred_element_type=F32)
                for mark in marks
            ],
            axis=0,
        ).astype(BF)
        pltpu.make_async_copy(m[f"raw{k}"], m[f"raw{k}"], m[f"raw_sem{k}"]).wait()
        flat = m[f"raw{k}"].reshape(BL, 4 * r, VB)

        per_cut = 4 // HALVES[k]

        def part(p, _):
            x = jnp.concatenate([flat[p * 4 + t] for t in range(4)], axis=1)
            lanes = pl.ds(pl.multiple_of(p * 4 * VB, 4 * VB), 4 * VB)
            got = matmul(order, x) * matmul(flags, expand[:, lanes])
            into = pl.ds(pl.multiple_of(p % per_cut * 4 * VB, 4 * VB), 4 * VB)
            for q in range(4):
                ma[q, p // per_cut, :, into] = got[q * r:(q + 1) * r].astype(BF)
            return 0

        lax.fori_loop(0, 4, part, 0, unroll=4 if k == 0 else 1)

    for k in CHUNKS:
        spread(k)
        if k == 0:
            pl.semaphore_wait(barrier, 16 - on_diag.astype(jnp.int32))
        plan = a_copies(k)
        for cut in range(HALVES[k]):
            for n in range(3):
                plan[n][cut].start()
        if k + 2 in CHUNKS:
            start_raw(k + 2)
        if k == 1:
            lax.fori_loop(0, NB, start_v, 0)

    v = m["v"]
    flags = keep[...].astype(BF)
    for n in range(NB):
        m["kx"][n] = matmul(flags, expand[:, n * NW:(n + 1) * NW])

    def mask_v(n, _):
        v_copy(n).wait()
        for b in range(BL):
            line = jnp.broadcast_to(m["kx"][n, b:b + 1, :], (16, NW)).astype(BF)
            rows = pl.ds(b * VB, VB)
            v[n, rows, :] = (v[n, rows, :].reshape(8, 16, NW) * line[None]).reshape(VB, NW)
        return 0

    lax.fori_loop(0, NB, mask_v, 0)

    def c_copy(g):
        return remote(m[f"cs{g}"], m[f"cr{g}"], m[f"c_ss{g}"], m[f"c_rs{g}"], sibling)

    def y_copies(g):
        return [
            remote(
                m[f"ys{g}"].at[:, (y + d) % 4], m[f"yr{g}"].at[d - 1],
                m[f"y_ss{g}"].at[d - 1], m[f"y_rs{g}"].at[d - 1], y_peer[d - 1],
            )
            for d in (1, 2, 3)
        ]

    def x_copies(g):
        plan = ((1 - xl, near),) if g == 0 else ((xl, far_same), (1 - xl, far_near))
        return [
            remote(
                m[f"xs{g}"].at[low], m[f"xr{g}"].at[n],
                m[f"x_ss{g}"].at[n], m[f"x_rs{g}"].at[n], peer,
            )
            for n, (low, peer) in enumerate(plan)
        ]

    def stack(pieces):
        if all(piece.shape[0] % 16 == 0 for piece in pieces):
            return jnp.concatenate(pieces, axis=0)
        return jnp.concatenate([p.astype(F32) for p in pieces], axis=0).astype(BF)

    def multiply(g):
        lhs, r = m[f"lhs{g}"], group_rows(g)
        if g == 0:
            pieces = []
            for k in CHUNKS:
                for copy in a_copies(k)[2]:
                    copy.wait_recv()
            for name, slot in (("ma", 2 * xh + c), ("got", 2)):
                for k in CHUNKS:
                    cuts = [m[f"{name}{k}"][slot, cut] for cut in range(HALVES[k])]
                    pieces.append(jnp.concatenate(cuts, axis=1))
            lhs[...] = stack(pieces)
        else:
            for k in GROUPS[g]:
                for n in range(2):
                    a_copies(k)[n][0].wait_recv()
            pieces = [m[f"got{k}"][n, 0] for n in range(2) for k in GROUPS[g]]
            lhs[:, :pieces[0].shape[1]] = stack(pieces)

        def column(n, _):
            got = matmul(lhs[...], v[n])
            m[f"pk{g}"][n // 4, n % 4] = got[:r]
            m[f"cs{g}"][n // 4, n % 4] = got[r:].astype(BF)
            return 0

        lax.fori_loop(0, NB, column, 0, unroll=1 if g == 0 else 2)
        c_copy(g).start()

    def vs_copy(n):
        return remote(v.at[n], m["vs"].at[n], m["vs_ss"].at[n], m["vs_rs"].at[n], sibling)

    def share_v(first):
        def start(n, _):
            vs_copy(first + n).start()
            return 0

        lax.fori_loop(0, NB // 2, start, 0)

    def wait_v():
        def wait(n, _):
            vs_copy(n).wait_recv()
            return 0

        lax.fori_loop(0, NB, wait, 0)

    def d_copies(g):
        return [
            remote(
                m[f"ds{g}"].at[(xl + b) % 2, (y + d) % 4], m[f"dr{g}"].at[b, d],
                m[f"d_ss{g}"].at[b, d], m[f"d_rs{g}"].at[b, d],
                dev(1 - xh, c, (xl + b) % 2, (y + d) % 4),
            )
            for b in range(2) for d in range(4)
        ]

    def multiply_whole(g):
        k = GROUPS[g][0]
        part, depth = m[f"part{g}"], W // HALVES[k]
        steps = [(cut, n) for cut in range(HALVES[k]) for n in range(2)]
        for at, (cut, n) in enumerate(steps):
            a_copies(k)[n][cut].wait_recv()
            weights = v if n == 0 else m["vs"]

            def column(b, _):
                got = matmul(m[f"got{k}"][n, cut], weights[b, cut * depth:(cut + 1) * depth, :])
                if at > 0:
                    got = got + part[b]
                if at < len(steps) - 1:
                    part[b] = got
                else:
                    m[f"ds{g}"][b // 4, b % 4] = got.astype(BF)
                return 0

            lax.fori_loop(0, NB, column, 0, unroll=2)
        for copy in d_copies(g):
            copy.start()

    def over_cores(g):
        pk, cr, ys = m[f"pk{g}"], m[f"cr{g}"], m[f"ys{g}"]
        c_copy(g).wait_recv()
        for low in range(2):
            for yy in range(4):
                both = pk[low, yy] + cr[low, yy].astype(F32)
                pk[low, yy] = both
                ys[low, yy] = both.astype(BF)
        for copy in y_copies(g):
            copy.start()

    def over_y(g):
        pk, yr, xt, xs = m[f"pk{g}"], m[f"yr{g}"], m[f"xt{g}"], m[f"xs{g}"]
        for copy in y_copies(g):
            copy.wait_recv()
        for low in range(2):
            both = pk[low, y]
            for d in range(3):
                both = both + yr[d, low].astype(F32)
            xt[low] = both
            xs[low] = both.astype(BF)
        for copy in x_copies(g):
            copy.start()

    total = m["total"]

    def over_x(g):
        if g == 0:
            x_copies(g)[0].wait_recv()
            total[...] = m["xt0"][xl] + m["xr0"][0].astype(F32)
            return
        first = STARTS[GROUPS[g][0]]
        rows = slice(first, first + group_rows(g))
        if g in DIRECT:
            for copy in d_copies(g):
                copy.wait_recv()
            terms = [m[f"dr{g}"][b, d] for b in range(2) for d in range(4)]
        else:
            for copy in x_copies(g):
                copy.wait_recv()
            terms = [m[f"xr{g}"][n] for n in range(2)]
        both = total[rows]
        for term in terms:
            both = both + term.astype(F32)
        total[rows] = both

    ts, tr = m["ts"], m["tr"]

    def t_copy(p, slot):
        h, first, rows = PIECES[p]
        return remote(
            ts.at[pl.ds(first, rows)], tr.at[slot, pl.ds(first, rows)],
            m["t_ss"].at[p], m["t_rs"].at[p, slot], turned[h],
        )

    def t_local(p):
        h, first, rows = PIECES[p]
        return pltpu.make_async_copy(
            ts.at[pl.ds(first, rows)], tr.at[h, pl.ds(first, rows)], m["t_ls"].at[p]
        )

    def t_mine(p):
        return jnp.logical_and(on_diag, here == PIECES[p][0])

    def ready(first, rows):
        ts[first:first + rows, :] = total[first:first + rows].astype(BF)

    def t_start(p):
        @pl.when(t_mine(p))
        def _():
            t_local(p).start()

        @pl.when(jnp.logical_not(t_mine(p)))
        def _():
            t_copy(p, here).start()

    def t_wait(p):
        block = PIECES[p][0]

        @pl.when(t_mine(p))
        def _():
            t_local(p).wait()

        @pl.when(jnp.logical_not(t_mine(p)))
        def _():
            t_copy(p, here).wait_send()

        for slot in (0, 1):
            there = jnp.logical_not(jnp.logical_and(on_diag, here == slot))

            @pl.when(jnp.logical_and(here == block, there))
            def _():
                t_copy(p, slot).wait_recv()

    def matrices():
        rt, ct = iota((ROWS, 2 * TB), 0), iota((ROWS, 2 * TB), 1)
        it = tenth(rt)
        jt = rt - 10 * it
        ht = jnp.where(it >= 10, 1, 0)
        m["turn"][...] = bits(ct == TB * ht + 4 * here + jt * 10 + it - 10 * ht)
        ts[ROWS - 8:TR, :] = jnp.zeros((16, NW), BF)

    multiply(0)
    share_v(0)
    matrices()
    over_cores(0)
    multiply(1)
    share_v(NB // 2)
    over_cores(1)
    over_y(0)
    multiply(2)
    over_y(1)
    over_cores(2)
    wait_v()
    multiply_whole(3)
    over_y(2)
    multiply_whole(4)
    over_x(0)
    over_x(1)
    over_x(2)
    ready(0, 144)
    t_start(0)
    t_start(1)
    over_x(3)
    over_x(4)
    ready(144, 56)
    t_start(2)

    for k in CHUNKS:
        for copies in a_copies(k):
            for copy in copies:
                copy.wait_send()
    for g in range(len(GROUPS)):
        for copy in d_copies(g) if g in DIRECT else [c_copy(g)] + y_copies(g) + x_copies(g):
            copy.wait_send()
    for n in range(NB):
        vs_copy(n).wait_send()
    for p in range(len(PIECES)):
        t_wait(p)

    rows = pl.ds(pl.multiple_of(TCUT * here, 16), TB)
    arrived = jnp.concatenate([tr[0, rows, :], tr[1, rows, :]], axis=0)
    across = matmul(m["turn"][...], arrived)
    odd = jnp.bitwise_and(iota((ROWS, NW), 1), 1) == 1
    across = jnp.where(odd, pltpu.roll(across, 1, 1), pltpu.roll(across, NW - 1, 1))
    both = total[...] + across
    for n in range(NW // VB):
        lanes = slice(n * VB, (n + 1) * VB)
        m["final"][n] = both[:, lanes]
        for j in range(10):
            out[j, :, lanes] = m["final"][n, pl.ds(j, 20, stride=10), :].astype(BF)


def shards(amplitude, integral, tile_mask, pair_irrep, slice_irrep, integral_mask):
    rows_i, rows_j, groups, _ = amplitude.shape
    tiles = amplitude.reshape(ROWS, groups, BL, VB).transpose(0, 2, 1, 3)
    hbm = pl.BlockSpec(memory_space=pltpu.HBM)
    vmem = pl.BlockSpec(memory_space=pltpu.VMEM)
    keep = (pair_irrep[0][:, None] == slice_irrep[None, :]) * integral_mask[0]
    result = pl.pallas_call(
        kernel,
        out_shape=jax.ShapeDtypeStruct((rows_j, rows_i, NW), BF),
        in_specs=[hbm, hbm, vmem, vmem],
        out_specs=pl.BlockSpec(memory_space=pltpu.VMEM),
        scratch_shapes=list(SCRATCH.values()),
        compiler_params=pltpu.CompilerParams(
            collective_id=0, has_side_effects=True, vmem_limit_bytes=52 * 2**20
        ),
        name="ladder",
    )(
        tiles, integral, tile_mask.transpose(1, 2, 0).astype(F32), keep.astype(F32),
    )
    return result.transpose(1, 0, 2)


def solution(mesh):
    placed = (
        P("occi", "occj", None, "virt"),
        P("occi", "virt", None),
        P("occi", None, "virt"),
        P("occi", "virt"),
        P(),
        P("occi", "virt", None),
    )
    return jax.shard_map(
        shards, mesh=mesh, in_specs=placed, out_specs=P("occi", "occj", "virt"), check_vma=False
    )
```

```python
import jax
import jax.numpy as jnp
from jax import lax
from jax.experimental import pallas as pl
from jax.experimental.pallas import tpu as pltpu
from jax.sharding import PartitionSpec as P

MESH = pl.DeviceIdType.MESH
BF = jnp.bfloat16
F32 = jnp.float32
ROWS = 200
SIZES = (16, 64, 64, 40, 16)
HALVES = (1, 1, 1, 1, 2)
STARTS = tuple(sum(SIZES[:k]) for k in range(len(SIZES)))
CHUNKS = range(len(SIZES))
GROUPS = ((), (0, 1), (2,), (3,), (4,))
DIRECT = (3, 4)
BL = 16
VB = 128
W = BL * VB
NB = 8
NW = 256
TR = 208
TB = 112
TCUT = 96
PIECES = ((0, 0, TB), (1, TCUT, 48), (1, 144, 64))
FROM_BOTH = tuple(k for g in DIRECT for k in GROUPS[g])


def group_rows(g):
    return ROWS if g == 0 else sum(SIZES[k] for k in GROUPS[g])


def iota(shape, axis):
    return lax.broadcasted_iota(jnp.int32, shape, axis)


def matmul(a, b):
    return jnp.dot(a, b, preferred_element_type=F32)


def bits(condition):
    return jnp.where(condition, 1.0, 0.0).astype(BF)


def tenth(x):
    return lax.shift_right_logical(x * 205, 11)


def scratch():
    dma = pltpu.SemaphoreType.DMA
    out = dict(
        v=pltpu.VMEM((NB, W, NW), BF),
        kx=pltpu.VMEM((NB, BL, NW), F32),
        expand=pltpu.VMEM((BL, W), BF),
        turn=pltpu.VMEM((ROWS, 2 * TB), BF),
        total=pltpu.VMEM((ROWS, NW), F32),
        final=pltpu.VMEM((NW // VB, ROWS, VB), F32),
        ts=pltpu.VMEM((TR, NW), BF),
        tr=pltpu.VMEM((2, TR, NW), BF),
        v_sem=dma((NB,)),
        t_ss=dma((3,)), t_rs=dma((3, 2)), t_ls=dma((3,)),
        vs=pltpu.VMEM((NB, W, NW), BF),
        vs_ss=dma((NB,)), vs_rs=dma((NB,)),
    )
    for k in CHUNKS:
        r = SIZES[k]
        out.update({
            f"raw{k}": pltpu.VMEM((BL, r, 4, VB), BF),
            f"ma{k}": pltpu.VMEM((4, HALVES[k], r, W // HALVES[k]), BF),
            f"got{k}": pltpu.VMEM((3, HALVES[k], r, W // HALVES[k]), BF),
            f"raw_sem{k}": dma, f"a_ss{k}": dma((3, 2)), f"a_rs{k}": dma((3, 2)),
        })
    for g in range(len(GROUPS)):
        r = group_rows(g)
        if g in DIRECT:
            out.update({
                f"part{g}": pltpu.VMEM((NB, r, NW), F32),
                f"ds{g}": pltpu.VMEM((2, 4, r, NW), BF),
                f"dr{g}": pltpu.VMEM((2, 4, r, NW), BF),
                f"d_ss{g}": dma((2, 4)), f"d_rs{g}": dma((2, 4)),
            })
            continue
        out.update({
            f"lhs{g}": pltpu.VMEM((2 * r, W), BF),
            f"pk{g}": pltpu.VMEM((2, 4, r, NW), F32),
            f"cs{g}": pltpu.VMEM((2, 4, r, NW), BF),
            f"cr{g}": pltpu.VMEM((2, 4, r, NW), BF),
            f"ys{g}": pltpu.VMEM((2, 4, r, NW), BF),
            f"yr{g}": pltpu.VMEM((3, 2, r, NW), BF),
            f"xt{g}": pltpu.VMEM((2, r, NW), F32),
            f"xs{g}": pltpu.VMEM((2, r, NW), BF),
            f"xr{g}": pltpu.VMEM((2, r, NW), BF),
            f"c_ss{g}": dma, f"c_rs{g}": dma,
            f"y_ss{g}": dma((3,)), f"y_rs{g}": dma((3,)),
            f"x_ss{g}": dma((2,)), f"x_rs{g}": dma((2,)),
        })
    return out


SCRATCH = scratch()


def kernel(amp, vint, tm, keep, out, *refs):
    m = dict(zip(SCRATCH, refs))
    occi, z, virt = lax.axis_index("occi"), lax.axis_index("occj"), lax.axis_index("virt")
    xh, c = occi // 2, occi % 2
    xl, y = virt // 4, virt % 4

    def dev(h, core, low, yy):
        return (2 * h + core, z, 4 * low + yy)

    sibling = dev(xh, 1 - c, xl, y)
    far_same = dev(1 - xh, c, xl, y)
    far_other = dev(1 - xh, 1 - c, xl, y)
    near = dev(xh, c, 1 - xl, y)
    far_near = dev(1 - xh, c, 1 - xl, y)
    y_peer = [dev(xh, c, xl, (y + d) % 4) for d in (1, 2, 3)]
    turned = [(z // 2, 2 * occi + h, virt) for h in (0, 1)]
    on_diag = (z // 2) == occi
    here = z % 2

    def remote(src, dst, send, recv, peer):
        return pltpu.make_async_remote_copy(
            src_ref=src, dst_ref=dst, send_sem=send, recv_sem=recv,
            device_id=peer, device_id_type=MESH,
        )

    def start_raw(k):
        def start(t, _):
            pltpu.make_async_copy(
                amp.at[pl.ds(STARTS[k], SIZES[k]), t], m[f"raw{k}"].at[t], m[f"raw_sem{k}"]
            ).start()
            return 0

        lax.fori_loop(0, BL, start, 0)

    def v_copy(n):
        return pltpu.make_async_copy(
            vint.at[0, :, pl.ds(pl.multiple_of(n * NW, NW), NW)], m["v"].at[n], m["v_sem"].at[n]
        )

    def start_v(n, _):
        v_copy(n).start()
        return 0

    start_raw(0)

    barrier = pltpu.get_barrier_semaphore()
    far = [dev(1 - xh, c, low, yy) for low in (0, 1) for yy in range(4)]
    for peer in far + [far_other, sibling, near] + y_peer:
        pl.semaphore_signal(barrier, inc=1, device_id=peer, device_id_type=MESH)
    for h in (0, 1):
        @pl.when(jnp.logical_not(jnp.logical_and(on_diag, here == h)))
        def _():
            pl.semaphore_signal(barrier, inc=1, device_id=turned[h], device_id_type=MESH)

    start_raw(1)

    expand = m["expand"]
    expand[...] = bits(lax.shift_right_logical(iota((BL, W), 1), 7) == iota((BL, W), 0))
    marks = [tm[q].astype(BF) for q in range(4)]

    def a_copies(k):
        far_q = 2 * (1 - xh)
        second = far_same if k in FROM_BOTH else far_other
        plan = ((far_q + c, far_same), (far_q + 1 - c, second), (2 * xh + 1 - c, sibling))
        return [
            [
                remote(
                    m[f"ma{k}"].at[q, cut], m[f"got{k}"].at[n, cut],
                    m[f"a_ss{k}"].at[n, cut], m[f"a_rs{k}"].at[n, cut], peer,
                )
                for cut in range(HALVES[k])
            ]
            for n, (q, peer) in enumerate(plan)
        ]

    def spread(k):
        r, ma = SIZES[k], m[f"ma{k}"]
        order = jnp.concatenate(
            [bits(iota((r, 4 * r), 1) == 4 * iota((r, 4 * r), 0) + q) for q in range(4)], axis=0
        )
        gap = iota((r, 20), 0) + STARTS[k] - 10 * iota((r, 20), 1)
        own_i = bits(jnp.logical_and(gap >= 0, gap < 10))
        flags = jnp.concatenate(
            [
                lax.dot_general(own_i, mark, (((1,), (1,)), ((), ())), preferred_element_type=F32)
                for mark in marks
            ],
            axis=0,
        ).astype(BF)
        pltpu.make_async_copy(m[f"raw{k}"], m[f"raw{k}"], m[f"raw_sem{k}"]).wait()
        flat = m[f"raw{k}"].reshape(BL, 4 * r, VB)

        per_cut = 4 // HALVES[k]

        def part(p, _):
            x = jnp.concatenate([flat[p * 4 + t] for t in range(4)], axis=1)
            lanes = pl.ds(pl.multiple_of(p * 4 * VB, 4 * VB), 4 * VB)
            got = matmul(order, x) * matmul(flags, expand[:, lanes])
            into = pl.ds(pl.multiple_of(p % per_cut * 4 * VB, 4 * VB), 4 * VB)
            for q in range(4):
                ma[q, p // per_cut, :, into] = got[q * r:(q + 1) * r].astype(BF)
            return 0

        lax.fori_loop(0, 4, part, 0, unroll=4 if k == 0 else 1)

    for k in CHUNKS:
        spread(k)
        if k == 0:
            pl.semaphore_wait(barrier, 16 - on_diag.astype(jnp.int32))
        plan = a_copies(k)
        for cut in range(HALVES[k]):
            for n in range(3):
                plan[n][cut].start()
        if k + 2 in CHUNKS:
            start_raw(k + 2)
        if k == 1:
            lax.fori_loop(0, NB, start_v, 0)

    v = m["v"]
    flags = keep[...].astype(BF)
    for n in range(NB):
        m["kx"][n] = matmul(flags, expand[:, n * NW:(n + 1) * NW])

    def mask_v(n, _):
        v_copy(n).wait()
        for b in range(BL):
            line = jnp.broadcast_to(m["kx"][n, b:b + 1, :], (16, NW)).astype(BF)
            rows = pl.ds(b * VB, VB)
            v[n, rows, :] = (v[n, rows, :].reshape(8, 16, NW) * line[None]).reshape(VB, NW)
        return 0

    lax.fori_loop(0, NB, mask_v, 0)

    def c_copy(g):
        return remote(m[f"cs{g}"], m[f"cr{g}"], m[f"c_ss{g}"], m[f"c_rs{g}"], sibling)

    def y_copies(g):
        return [
            remote(
                m[f"ys{g}"].at[:, (y + d) % 4], m[f"yr{g}"].at[d - 1],
                m[f"y_ss{g}"].at[d - 1], m[f"y_rs{g}"].at[d - 1], y_peer[d - 1],
            )
            for d in (1, 2, 3)
        ]

    def x_copies(g):
        plan = ((1 - xl, near),) if g == 0 else ((xl, far_same), (1 - xl, far_near))
        return [
            remote(
                m[f"xs{g}"].at[low], m[f"xr{g}"].at[n],
                m[f"x_ss{g}"].at[n], m[f"x_rs{g}"].at[n], peer,
            )
            for n, (low, peer) in enumerate(plan)
        ]

    def stack(pieces):
        if all(piece.shape[0] % 16 == 0 for piece in pieces):
            return jnp.concatenate(pieces, axis=0)
        return jnp.concatenate([p.astype(F32) for p in pieces], axis=0).astype(BF)

    def multiply(g):
        lhs, r = m[f"lhs{g}"], group_rows(g)
        if g == 0:
            pieces = []
            for k in CHUNKS:
                for copy in a_copies(k)[2]:
                    copy.wait_recv()
            for name, slot in (("ma", 2 * xh + c), ("got", 2)):
                for k in CHUNKS:
                    cuts = [m[f"{name}{k}"][slot, cut] for cut in range(HALVES[k])]
                    pieces.append(jnp.concatenate(cuts, axis=1))
            lhs[...] = stack(pieces)
        else:
            for k in GROUPS[g]:
                for n in range(2):
                    a_copies(k)[n][0].wait_recv()
            pieces = [m[f"got{k}"][n, 0] for n in range(2) for k in GROUPS[g]]
            lhs[:, :pieces[0].shape[1]] = stack(pieces)

        def column(n, _):
            got = matmul(lhs[...], v[n])
            m[f"pk{g}"][n // 4, n % 4] = got[:r]
            m[f"cs{g}"][n // 4, n % 4] = got[r:].astype(BF)
            return 0

        lax.fori_loop(0, NB, column, 0, unroll=1 if g == 0 else 2)
        c_copy(g).start()

    def vs_copy(n):
        return remote(v.at[n], m["vs"].at[n], m["vs_ss"].at[n], m["vs_rs"].at[n], sibling)

    def share_v(first):
        def start(n, _):
            vs_copy(first + n).start()
            return 0

        lax.fori_loop(0, NB // 2, start, 0)

    def wait_v():
        def wait(n, _):
            vs_copy(n).wait_recv()
            return 0

        lax.fori_loop(0, NB, wait, 0)

    def d_copies(g):
        return [
            remote(
                m[f"ds{g}"].at[(xl + b) % 2, (y + d) % 4], m[f"dr{g}"].at[b, d],
                m[f"d_ss{g}"].at[b, d], m[f"d_rs{g}"].at[b, d],
                dev(1 - xh, c, (xl + b) % 2, (y + d) % 4),
            )
            for b in range(2) for d in range(4)
        ]

    def multiply_whole(g):
        k = GROUPS[g][0]
        part, depth = m[f"part{g}"], W // HALVES[k]
        steps = [(cut, n) for cut in range(HALVES[k]) for n in range(2)]
        for at, (cut, n) in enumerate(steps):
            a_copies(k)[n][cut].wait_recv()
            weights = v if n == 0 else m["vs"]

            def column(b, _):
                got = matmul(m[f"got{k}"][n, cut], weights[b, cut * depth:(cut + 1) * depth, :])
                if at > 0:
                    got = got + part[b]
                if at < len(steps) - 1:
                    part[b] = got
                else:
                    m[f"ds{g}"][b // 4, b % 4] = got.astype(BF)
                return 0

            lax.fori_loop(0, NB, column, 0, unroll=2)
        for copy in d_copies(g):
            copy.start()

    def over_cores(g):
        pk, cr, ys = m[f"pk{g}"], m[f"cr{g}"], m[f"ys{g}"]
        c_copy(g).wait_recv()
        for low in range(2):
            for yy in range(4):
                both = pk[low, yy] + cr[low, yy].astype(F32)
                pk[low, yy] = both
                ys[low, yy] = both.astype(BF)
        for copy in y_copies(g):
            copy.start()

    def over_y(g):
        pk, yr, xt, xs = m[f"pk{g}"], m[f"yr{g}"], m[f"xt{g}"], m[f"xs{g}"]
        for copy in y_copies(g):
            copy.wait_recv()
        for low in range(2):
            both = pk[low, y]
            for d in range(3):
                both = both + yr[d, low].astype(F32)
            xt[low] = both
            xs[low] = both.astype(BF)
        for copy in x_copies(g):
            copy.start()

    total = m["total"]

    def over_x(g):
        if g == 0:
            x_copies(g)[0].wait_recv()
            total[...] = m["xt0"][xl] + m["xr0"][0].astype(F32)
            return
        first = STARTS[GROUPS[g][0]]
        rows = slice(first, first + group_rows(g))
        if g in DIRECT:
            for copy in d_copies(g):
                copy.wait_recv()
            terms = [m[f"dr{g}"][b, d] for b in range(2) for d in range(4)]
        else:
            for copy in x_copies(g):
                copy.wait_recv()
            terms = [m[f"xr{g}"][n] for n in range(2)]
        both = total[rows]
        for term in terms:
            both = both + term.astype(F32)
        total[rows] = both

    ts, tr = m["ts"], m["tr"]

    def t_copy(p, slot):
        h, first, rows = PIECES[p]
        return remote(
            ts.at[pl.ds(first, rows)], tr.at[slot, pl.ds(first, rows)],
            m["t_ss"].at[p], m["t_rs"].at[p, slot], turned[h],
        )

    def t_local(p):
        h, first, rows = PIECES[p]
        return pltpu.make_async_copy(
            ts.at[pl.ds(first, rows)], tr.at[h, pl.ds(first, rows)], m["t_ls"].at[p]
        )

    def t_mine(p):
        return jnp.logical_and(on_diag, here == PIECES[p][0])

    def ready(first, rows):
        ts[first:first + rows, :] = total[first:first + rows].astype(BF)

    def t_start(p):
        @pl.when(t_mine(p))
        def _():
            t_local(p).start()

        @pl.when(jnp.logical_not(t_mine(p)))
        def _():
            t_copy(p, here).start()

    def t_wait(p):
        block = PIECES[p][0]

        @pl.when(t_mine(p))
        def _():
            t_local(p).wait()

        @pl.when(jnp.logical_not(t_mine(p)))
        def _():
            t_copy(p, here).wait_send()

        for slot in (0, 1):
            there = jnp.logical_not(jnp.logical_and(on_diag, here == slot))

            @pl.when(jnp.logical_and(here == block, there))
            def _():
                t_copy(p, slot).wait_recv()

    def matrices():
        rt, ct = iota((ROWS, 2 * TB), 0), iota((ROWS, 2 * TB), 1)
        it = tenth(rt)
        jt = rt - 10 * it
        ht = jnp.where(it >= 10, 1, 0)
        m["turn"][...] = bits(ct == TB * ht + 4 * here + jt * 10 + it - 10 * ht)
        ts[ROWS - 8:TR, :] = jnp.zeros((16, NW), BF)

    multiply(0)
    share_v(0)
    matrices()
    over_cores(0)
    multiply(1)
    share_v(NB // 2)
    over_cores(1)
    over_y(0)
    multiply(2)
    over_y(1)
    over_cores(2)
    wait_v()
    multiply_whole(3)
    over_y(2)
    multiply_whole(4)
    over_x(0)
    over_x(1)
    over_x(2)
    ready(0, 144)
    t_start(1)
    t_start(0)
    over_x(3)
    over_x(4)
    ready(144, 56)
    t_start(2)

    for k in CHUNKS:
        for copies in a_copies(k):
            for copy in copies:
                copy.wait_send()
    for g in range(len(GROUPS)):
        for copy in d_copies(g) if g in DIRECT else [c_copy(g)] + y_copies(g) + x_copies(g):
            copy.wait_send()
    for n in range(NB):
        vs_copy(n).wait_send()
    for p in range(len(PIECES)):
        t_wait(p)

    rows = pl.ds(pl.multiple_of(TCUT * here, 16), TB)
    arrived = jnp.concatenate([tr[0, rows, :], tr[1, rows, :]], axis=0)
    across = matmul(m["turn"][...], arrived)
    odd = jnp.bitwise_and(iota((ROWS, NW), 1), 1) == 1
    across = jnp.where(odd, pltpu.roll(across, 1, 1), pltpu.roll(across, NW - 1, 1))
    both = total[...] + across
    for n in range(NW // VB):
        lanes = slice(n * VB, (n + 1) * VB)
        m["final"][n] = both[:, lanes]
        for j in range(10):
            out[j, :, lanes] = m["final"][n, pl.ds(j, 20, stride=10), :].astype(BF)


def shards(amplitude, integral, tile_mask, pair_irrep, slice_irrep, integral_mask):
    rows_i, rows_j, groups, _ = amplitude.shape
    tiles = amplitude.reshape(ROWS, groups, BL, VB).transpose(0, 2, 1, 3)
    hbm = pl.BlockSpec(memory_space=pltpu.HBM)
    vmem = pl.BlockSpec(memory_space=pltpu.VMEM)
    keep = (pair_irrep[0][:, None] == slice_irrep[None, :]) * integral_mask[0]
    result = pl.pallas_call(
        kernel,
        out_shape=jax.ShapeDtypeStruct((rows_j, rows_i, NW), BF),
        in_specs=[hbm, hbm, vmem, vmem],
        out_specs=pl.BlockSpec(memory_space=pltpu.VMEM),
        scratch_shapes=list(SCRATCH.values()),
        compiler_params=pltpu.CompilerParams(
            collective_id=0, has_side_effects=True, vmem_limit_bytes=52 * 2**20
        ),
        name="ladder",
    )(
        tiles, integral, tile_mask.transpose(1, 2, 0).astype(F32), keep.astype(F32),
    )
    return result.transpose(1, 0, 2)


def solution(mesh):
    placed = (
        P("occi", "occj", None, "virt"),
        P("occi", "virt", None),
        P("occi", None, "virt"),
        P("occi", "virt"),
        P(),
        P("occi", "virt", None),
    )
    return jax.shard_map(
        shards, mesh=mesh, in_specs=placed, out_specs=P("occi", "occj", "virt"), check_vma=False
    )
```
